512 devices in a mesh: grp: 16 (over y_hi, x, core), chan: 32 (over y_lo, z).
Axes of the slice: x: 4, y: 8 (y_hi: 2, y_lo: 4; y = y_hi * 4 + y_lo), z: 8, core: 2. Of those that a mesh axis runs over, the one named last changes fastest.
Arguments:
- voltages: int32 [1024, 31, 8192], P('grp', None, 'chan'), may hold values from -128 to 127
- plan: int32 [3, 16], replicated, may hold values from 0 to 15, as said below
Outputs:
- visibility: bfloat16 [3, 1024, 2048, 128], P(None, 'grp', 'chan')
The draws below stay inside these ranges and needn't reach their ends.
Inputs may be any that keep to these rules, and one draw needn't show every extreme that they name: Every row is a perfect matching of the 16 groups: plan[r, plan[r, g]] = g and plan[r, g] != g; the 3 partners of a group are all different.
All inputs are finite; a program needn't handle non-finite values.
Results may differ from the reference program's by a relative error of at most 0.0057.
Values may be sent and summed in bfloat16 or wider, within the bound.
A program may use at most 64 MiB of HBM per device.

```python
import math
import jax
import jax.numpy as jnp
from jax import lax

SIG = 64
CH = 4096
TAPS = 16
SPEC = 16
ROUNDS = 3
GROUPS = 16
NSIG = 1024
NFFT = 8192
FRAMES = 31
HALF = 64
HALF_ALL = 2048
N_CHAN = 32


def draw_plan(key, part):
    key_teams = jax.random.fold_in(key, 4099)
    key_rounds = jax.random.fold_in(key, 7919)
    labels = jax.random.permutation(key_teams, GROUPS)
    chosen = jax.random.permutation(key_rounds, GROUPS - 1)[:ROUNDS]
    team_ids = jnp.arange(GROUPS)
    last_team = GROUPS - 1

    def one_round(round_index):
        opposite = (2 * round_index - team_ids) % last_team
        team_partner = jnp.where(team_ids == last_team, round_index, jnp.where(team_ids == round_index, last_team, opposite))
        return jnp.zeros((GROUPS,), jnp.int32).at[labels].set(labels[team_partner].astype(jnp.int32))
    return jax.vmap(one_round)(chosen).astype(jnp.int32)


def place_ends(entries, stream_key, low, high):
    shape = entries.shape
    index_at = [jax.random.randint(jax.random.fold_in(stream_key, axis), (), 0, shape[axis]) for axis in range(len(shape))]
    entries = entries.at[tuple(index_at)].set(low)
    longest = shape.index(max(shape))
    index_at[longest] = (index_at[longest] + 1) % shape[longest]
    return entries.at[tuple(index_at)].set(high)


def setup_inputs(seed: int = 0) -> dict:
    key_of = jax.random.split(jax.random.key(seed), 3)
    voltages = place_ends(jax.random.randint(key_of[0], (NSIG, FRAMES, NFFT), -128, 128), jax.random.fold_in(key_of[0], 1), -128, 127).astype(jnp.int32)
    plan = draw_plan(jax.random.fold_in(key_of[2], 71), 0)
    return dict(voltages=voltages, plan=plan)


def taper_coeff(position, length_total, fft_len):
    window = 0.5 - 0.5 * jnp.cos(2.0 * math.pi * position / length_total)
    return window * jnp.sinc((position - 0.5 * length_total) / fft_len)

def reference(voltages, plan):
    fft_len = 2 * CH
    samples = voltages.astype(jnp.float32)
    positions = jnp.arange(TAPS * fft_len).astype(jnp.float32)
    coeffs = taper_coeff(positions, TAPS * fft_len, fft_len).reshape(TAPS, fft_len)
    filtered = jnp.zeros((NSIG, SPEC, fft_len), jnp.float32)
    for tap_index in range(TAPS):
        filtered = filtered + coeffs[tap_index] * samples[:, tap_index:tap_index + SPEC, :]
    spectra = jnp.fft.rfft(filtered, axis=-1)[..., :CH] * (1.0 / (64.0 * math.sqrt(fft_len)))
    chan_re = lax.optimization_barrier(jnp.real(spectra).astype(jnp.bfloat16)).astype(jnp.float32)
    chan_im = lax.optimization_barrier(jnp.imag(spectra).astype(jnp.bfloat16)).astype(jnp.float32)
    chan_pos = jnp.arange(HALF_ALL)
    device_of = chan_pos // HALF
    inner_pos = chan_pos % HALF
    low_index = (device_of + N_CHAN * inner_pos).astype(jnp.int32)
    high_index = (device_of + N_CHAN * (inner_pos + HALF)).astype(jnp.int32)

    def one_pair(pair_index):
        round_index = pair_index // GROUPS
        group_index = pair_index % GROUPS
        partner = plan[round_index, group_index]
        chosen = jnp.where(group_index > partner, high_index, low_index)

        def pick(data, group):
            rows = lax.dynamic_slice_in_dim(data, (group * SIG).astype(jnp.int32), SIG, 0)
            return jnp.take(rows, chosen, axis=2)
        mine_re = pick(chan_re, group_index)
        mine_im = pick(chan_im, group_index)
        other_re = pick(chan_re, partner)
        other_im = pick(chan_im, partner)
        vis_re = jnp.einsum('asq,bsq->aqb', mine_re, other_re) + jnp.einsum('asq,bsq->aqb', mine_im, other_im)
        vis_im = jnp.einsum('asq,bsq->aqb', mine_im, other_re) - jnp.einsum('asq,bsq->aqb', mine_re, other_im)
        return (jnp.concatenate([vis_re, vis_im], axis=-1) / SPEC).astype(jnp.bfloat16)
    stacked = lax.map(one_pair, jnp.arange(ROUNDS * GROUPS, dtype=jnp.int32))
    return stacked.reshape(ROUNDS, NSIG, HALF_ALL, 2 * SIG)
```

```python
import functools
import math

import jax
import jax.numpy as jnp
import numpy as np
from jax import lax
from jax.experimental import pallas as pl
from jax.experimental.pallas import tpu as pltpu
from jax.sharding import PartitionSpec as P

TAPS = 16
MESH = pl.DeviceIdType.MESH
F32 = jnp.float32
BF16 = jnp.bfloat16


def coeff_table(fft_len, n_chan):
    position = np.arange(TAPS * fft_len, dtype=np.float64)
    length = TAPS * fft_len
    window = 0.5 - 0.5 * np.cos(2.0 * np.pi * position / length)
    coeff = window * np.sinc((position - 0.5 * length) / fft_len)
    block = fft_len // n_chan
    table = coeff.reshape(TAPS, n_chan, block).transpose(1, 0, 2)
    return np.ascontiguousarray(table.astype(np.float32))


def twiddle_table(fft_len, n_chan):
    block = fft_len // n_chan
    c = np.arange(n_chan // 2 + 1)[:, None]
    m = np.arange(block)[None, :]
    angle = 2.0 * np.pi * (c * m) / fft_len
    return np.stack([np.cos(angle), np.sin(angle)], 1).astype(np.float32)


def second_matrix(fft_len, block):
    half = block // 4
    m = np.arange(block)[:, None]
    j = np.arange(block // 2)[None, :]
    theta = 2.0 * np.pi * (m * j % block) / block
    phi = 2.0 * np.pi * (m * (j + 1) % block) / block
    re = np.concatenate([np.cos(theta), np.sin(theta)], 0)
    im = np.concatenate([-np.sin(theta), np.cos(theta)], 0)
    re_mirror = np.concatenate([np.cos(phi), -np.sin(phi)], 0)
    im_mirror = np.concatenate([-np.sin(phi), -np.cos(phi)], 0)
    parts = []
    for real, imag in ((re, im), (re_mirror, im_mirror)):
        for lo in (0, half):
            parts.append(real[:, lo : lo + half])
            parts.append(imag[:, lo : lo + half])
    full = np.concatenate(parts, 1) / (64.0 * math.sqrt(fft_len))
    high = full.astype(np.float32).astype(BF16)
    low = (full - high.astype(np.float64)).astype(np.float32).astype(BF16)
    return high, low


def real_dft(x):
    n = len(x)
    if n == 1:
        return [(x[0], None)]
    if n == 2:
        return [(x[0] + x[1], None), (x[0] - x[1], None)]
    even = real_dft(x[0::2])
    odd = real_dft(x[1::2])
    out = [None] * (n // 2 + 1)
    out[0] = (even[0][0] + odd[0][0], None)
    out[n // 2] = (even[0][0] - odd[0][0], None)
    quarter = n // 4
    out[quarter] = (even[quarter][0], -odd[quarter][0])
    for c in range(1, quarter):
        er, ei = even[c]
        orr, oi = odd[c]
        angle = 2.0 * math.pi * c / n
        wr, wi = math.cos(angle), -math.sin(angle)
        if 8 * c == n:
            tr, ti = (orr + oi) * wr, (oi - orr) * wr
        else:
            tr, ti = orr * wr - oi * wi, orr * wi + oi * wr
        out[c] = (er + tr, ei + ti)
        out[n // 2 - c] = (er - tr, ti - ei)
    return out


def exchange_kernel(
    dims,
    v_ref, coeff_ref, tw_ref, bh_ref, bl_ref,
    own_ref, slots_ref,
    coeff, filt, r1, zh, zl, s2, r2, r2x, t32, t32x, tn, tx,
    coeff_sem, send1, recv1, send2, recv2, send2x, recv2x, local_sem, sendq, recvq, relay_sem, relayq,
):
    n_chan, plane, sig, spec, block = dims
    me = lax.axis_index("chan")
    gid = lax.axis_index("grp")
    other = lax.rem(gid + plane, 2 * plane)
    y_hi = gid // plane
    x = lax.rem(gid, plane) // 2
    core = lax.rem(gid, 2)
    n_x = plane // 2
    sib = y_hi * plane + x * 2 + (1 - core)
    barrier = pltpu.get_barrier_semaphore()

    def greet(k, carry):
        peer = lax.rem(me + k, n_chan)

        @pl.when(k > 0)
        def _():
            pl.semaphore_signal(barrier, inc=1, device_id={"chan": peer}, device_id_type=MESH)

        pl.semaphore_signal(
            barrier, inc=1, device_id={"grp": other, "chan": peer}, device_id_type=MESH
        )
        return carry

    lax.fori_loop(0, n_chan, greet, 0)
    for dx in range(1, n_x):
        dest = y_hi * plane + lax.rem(x + dx, n_x) * 2 + core
        pl.semaphore_signal(barrier, inc=1, device_id={"grp": dest}, device_id_type=MESH)
    pl.semaphore_signal(barrier, inc=1, device_id={"grp": sib}, device_id_type=MESH)

    load = pltpu.make_async_copy(coeff_ref.at[me], coeff, coeff_sem)
    load.start()
    load.wait()

    def fir(s, carry):
        for lane in range(0, block, 128):
            lanes = pl.ds(lane, 128)
            total = None
            for t in range(TAPS):
                term = coeff[t : t + 1, lanes] * v_ref[s + t, :, lanes]
                total = term if total is None else total + term
            filt[2 * s, :, lanes] = total[: sig // 2].astype(BF16)
            filt[2 * s + 1, :, lanes] = total[sig // 2 :].astype(BF16)
        return carry

    lax.fori_loop(0, spec, fir, 0)
    pl.semaphore_wait(barrier, 2 * n_chan - 1 + n_x)

    def copy1(src, dest):
        return pltpu.make_async_remote_copy(
            src_ref=filt.at[dest], dst_ref=r1.at[src], send_sem=send1.at[dest], recv_sem=recv1.at[src],
            device_id={"chan": dest}, device_id_type=MESH,
        )

    def start1(k, carry):
        copy1(me, lax.rem(me + k, n_chan)).start()
        return carry

    lax.fori_loop(1, n_chan, start1, 0)
    mine1 = pltpu.make_async_copy(filt.at[me], r1.at[me], local_sem.at[0])
    mine1.start()
    mine1.wait()

    def wait1(k, carry):
        peer = lax.rem(me + k, n_chan)
        copy1(peer, peer).wait_recv()
        return carry

    lax.fori_loop(1, n_chan, wait1, 0)

    rows = sig * spec // n_chan
    n_half = n_chan // 2

    def first(p, carry):
        row = pl.multiple_of((p // 2) * 16, 16)
        lane = pl.multiple_of(lax.rem(p, 2) * 128, 128)
        samples = [r1[d, pl.ds(row, 16), pl.ds(lane, 128)].astype(F32) for d in range(n_chan)]
        for c, (re, im) in enumerate(real_dft(samples)):
            cos = tw_ref[c, 0:1, pl.ds(lane, 128)]
            sin = tw_ref[c, 1:2, pl.ds(lane, 128)]
            if im is None:
                zr, zi = re * cos, -(re * sin)
            else:
                zr, zi = re * cos + im * sin, im * cos - re * sin
            for base, z in ((0, zr), (block, zi)):
                lanes = pl.ds(pl.multiple_of(base + lane, 128), 128)
                high = z.astype(BF16)
                zh[c, pl.ds(row, 16), lanes] = high
                zl[c, pl.ds(row, 16), lanes] = (z - high.astype(F32)).astype(BF16)
        return carry

    lax.fori_loop(0, (rows // 16) * (block // 128), first, 0)

    for lo, hi in ((0, n_half // 2 + 1), (n_half // 2 + 1, n_half + 1)):
        count = (hi - lo) * rows
        left_h = zh[lo:hi].reshape(count, 2 * block)
        left_l = zl[lo:hi].reshape(count, 2 * block)
        out = jnp.dot(left_h, bh_ref[...], preferred_element_type=F32)
        out += jnp.dot(left_h, bl_ref[...], preferred_element_type=F32)
        out += jnp.dot(left_l, bh_ref[...], preferred_element_type=F32)
        for c in range(lo, hi):
            part = out[(c - lo) * rows : (c - lo + 1) * rows].astype(BF16)
            s2[c, 0] = part[:, 0:128]
            s2[c, 1] = part[:, 128:256]
            if 0 < c < n_half:
                s2[n_chan - c, 0] = part[:, 256:384]
                s2[n_chan - c, 1] = part[:, 384:512]

    def copy2(src, dest):
        return pltpu.make_async_remote_copy(
            src_ref=s2.at[dest], dst_ref=r2.at[src], send_sem=send2.at[dest], recv_sem=recv2.at[src],
            device_id={"chan": dest}, device_id_type=MESH,
        )

    def copy2x(src, dest):
        return pltpu.make_async_remote_copy(
            src_ref=s2.at[dest, 1 - y_hi], dst_ref=r2x.at[src],
            send_sem=send2x.at[dest], recv_sem=recv2x.at[src],
            device_id={"grp": other, "chan": dest}, device_id_type=MESH,
        )

    def start2(k, carry):
        dest = lax.rem(me + k, n_chan)

        @pl.when(k > 0)
        def _():
            copy2(me, dest).start()

        copy2x(me, dest).start()
        return carry

    lax.fori_loop(0, n_chan, start2, 0)
    mine2 = pltpu.make_async_copy(s2.at[me], r2.at[me], local_sem.at[0])
    mine2.start()
    mine2.wait()

    def wait2(k, carry):
        peer = lax.rem(me + k, n_chan)
        copy2(peer, peer).wait_recv()
        return carry

    lax.fori_loop(1, n_chan, wait2, 0)
    low_lane = lax.broadcasted_iota(jnp.int32, (sig, 128), 1) < 64

    def swap(a, b):
        re = jnp.where(low_lane, a, pltpu.roll(b, 64, 1))
        im = jnp.where(low_lane, pltpu.roll(a, 64, 1), b)
        return jnp.concatenate([re, im], 0).T

    def turn(s, carry):
        low = r2[pl.ds(2 * s, 2), 0].reshape(sig, 128).astype(F32)
        high = r2[pl.ds(2 * s, 2), 1].reshape(sig, 128).astype(F32)
        t32[pl.ds(s, 128, stride=spec), :] = swap(low, high)
        return carry

    lax.fori_loop(0, spec, turn, 0)

    def pack(i, carry):
        row = pl.multiple_of(i * 128, 128)
        tn[pl.ds(i * 8, 8)] = t32[pl.ds(row, 128), :].reshape(8, spec, 128).astype(BF16)
        return carry

    lax.fori_loop(0, 16, pack, 0)

    def copyq(src_ref, slot, sem, dest_grp):
        return pltpu.make_async_remote_copy(
            src_ref=src_ref, dst_ref=slots_ref.at[slot], send_sem=sem, recv_sem=recvq.at[slot],
            device_id={"grp": dest_grp}, device_id_type=MESH,
        )

    sends = []
    for dx in range(1, n_x):
        dest_x = lax.rem(x + dx, n_x)
        dest = y_hi * plane + dest_x * 2 + core
        upper = (dest_x > x).astype(jnp.int32)
        sends.append(copyq(tn.at[pl.ds(upper * 64, 64)], gid, sendq.at[dx - 1], dest))
        sends[-1].start()
    sends.append(copyq(tn.at[pl.ds((1 - core) * 64, 64)], gid, sendq.at[n_x - 1], sib))
    sends[-1].start()
    keep = pltpu.make_async_copy(tn, own_ref, local_sem.at[0])
    keep.start()

    def wait2x(k, carry):
        peer = lax.rem(me + k, n_chan)
        copy2x(peer, peer).wait_recv()
        return carry

    lax.fori_loop(0, n_chan, wait2x, 0)

    def turnx(i, carry):
        first_s = r2x[pl.ds(4 * i, 2)].reshape(sig, 128).astype(F32)
        second_s = r2x[pl.ds(4 * i + 2, 2)].reshape(sig, 128).astype(F32)
        both = swap(first_s, second_s)
        t32x[pl.ds(2 * i, 64, stride=spec), :] = both[:64]
        t32x[pl.ds(2 * i + 1, 64, stride=spec), :] = both[64:]
        return carry

    lax.fori_loop(0, spec // 2, turnx, 0)

    def packx(i, carry):
        row = pl.multiple_of(i * 128, 128)
        tx[pl.ds(i * 8, 8)] = t32x[pl.ds(row, 128), :].reshape(8, spec, 128).astype(BF16)
        return carry

    lax.fori_loop(0, 8, packx, 0)
    for dx in range(1, n_x):
        dest = y_hi * plane + lax.rem(x + dx, n_x) * 2 + core
        sends.append(copyq(tx, other, sendq.at[n_x + dx - 1], dest))
        sends[-1].start()
    sends.append(copyq(tx, other, sendq.at[2 * n_x - 1], sib))
    sends[-1].start()
    keepx = pltpu.make_async_copy(tx, slots_ref.at[other], local_sem.at[1])
    keepx.start()

    relays = []
    for part in range(2):
        for dx in range(1, n_x):
            source = lax.rem(y_hi + part, 2) * plane + lax.rem(x + n_x - dx, n_x) * 2 + core
            copyq(tx, source, sendq.at[0], sib).wait_recv()
            relays.append(copyq(slots_ref.at[source], source, relay_sem.at[part * (n_x - 1) + dx - 1], sib))
            relays[-1].start()
    for part in range(2):
        for dx in range(n_x):
            slot = lax.rem(y_hi + part, 2) * plane + lax.rem(x + dx, n_x) * 2 + (1 - core)
            copyq(tx, slot, sendq.at[0], sib).wait_recv()
    keep.wait()
    keepx.wait()
    for item in sends + relays:
        item.wait_send()

    def drain(k, carry):
        dest = lax.rem(me + k, n_chan)

        @pl.when(k > 0)
        def _():
            copy1(me, dest).wait_send()
            copy2(me, dest).wait_send()

        copy2x(me, dest).wait_send()
        return carry

    lax.fori_loop(0, n_chan, drain, 0)


def correlate_kernel(spec, pick_ref, own_ref, other_ref, out_ref, total):
    count = own_ref.shape[0]
    low_lane = lax.broadcasted_iota(jnp.int32, (spec, 128), 1) < 64
    for j in range(count):
        mine = own_ref[j].astype(F32)
        theirs = other_ref[0, j].astype(F32)
        left = jnp.concatenate([mine, pltpu.roll(mine, 64, 1)], 0)[:, :64].astype(BF16)
        right = jnp.concatenate(
            [jnp.where(low_lane, theirs, -theirs), pltpu.roll(theirs, 64, 1)], 0
        ).astype(BF16)
        product = lax.dot_general(left, right, (((0,), (0,)), ((), ())), preferred_element_type=F32)
        total[pl.ds(j, 64, stride=count), :] = product * (1.0 / spec)
    out_ref[0] = total[...].reshape(64, count, 128).astype(BF16)


def solution(mesh):
    n_chan = mesh.shape["chan"]
    n_grp = mesh.shape["grp"]
    plane = n_grp // 2
    n_x = plane // 2

    def local(voltages, plan):
        sig, frames, block = voltages.shape
        spec = frames - TAPS + 1
        fft_len = block * n_chan
        rows = sig * spec // n_chan
        n_c = n_chan // 2 + 1
        rounds = plan.shape[0]
        table = jnp.asarray(coeff_table(fft_len, n_chan))
        twiddle = jnp.asarray(twiddle_table(fft_len, n_chan))
        high, low = second_matrix(fft_len, block)
        frames_first = voltages.transpose(1, 0, 2).astype(F32)
        vmem = pl.BlockSpec(memory_space=pltpu.VMEM)
        anyspace = pl.BlockSpec(memory_space=pl.ANY)
        dma = pltpu.SemaphoreType.DMA
        own, slots = pl.pallas_call(
            functools.partial(exchange_kernel, (n_chan, plane, sig, spec, block)),
            out_shape=(
                jax.ShapeDtypeStruct((128, spec, 128), BF16),
                jax.ShapeDtypeStruct((n_grp, 64, spec, 128), BF16),
            ),
            in_specs=[vmem, anyspace, vmem, vmem, vmem],
            out_specs=(anyspace, anyspace),
            scratch_shapes=[
                pltpu.VMEM((TAPS, block), F32),
                pltpu.VMEM((n_chan, rows, block), BF16),
                pltpu.VMEM((n_chan, rows, block), BF16),
                pltpu.VMEM((n_c, rows, 2 * block), BF16),
                pltpu.VMEM((n_c, rows, 2 * block), BF16),
                pltpu.VMEM((n_chan, 2, rows, 128), BF16),
                pltpu.VMEM((n_chan, 2, rows, 128), BF16),
                pltpu.VMEM((n_chan, rows, 128), BF16),
                pltpu.VMEM((128 * spec, 128), F32),
                pltpu.VMEM((64 * spec, 128), F32),
                pltpu.VMEM((128, spec, 128), BF16),
                pltpu.VMEM((64, spec, 128), BF16),
                dma, dma((n_chan,)), dma((n_chan,)), dma((n_chan,)), dma((n_chan,)),
                dma((n_chan,)), dma((n_chan,)), dma((2,)), dma((2 * n_x,)), dma((n_grp,)),
                dma((2 * n_x,)), dma,
            ],
            compiler_params=pltpu.CompilerParams(
                collective_id=0, has_side_effects=True, vmem_limit_bytes=48 * 1024 * 1024
            ),
            cost_estimate=pl.CostEstimate(
                flops=10**9, bytes_accessed=10**7, transcendentals=0
            ),
        )(frames_first, table, twiddle, jnp.asarray(high), jnp.asarray(low))
        gid = lax.axis_index("grp")
        partner = lax.dynamic_index_in_dim(plan, gid, 1, keepdims=False)
        pick = jnp.stack([partner, (gid > partner).astype(jnp.int32)])
        step = 16
        return pl.pallas_call(
            functools.partial(correlate_kernel, spec),
            out_shape=jax.ShapeDtypeStruct((rounds, sig, 64, 2 * sig), BF16),
            grid_spec=pltpu.PrefetchScalarGridSpec(
                num_scalar_prefetch=1,
                grid=(rounds, 64 // step),
                in_specs=[
                    pl.BlockSpec((step, spec, 128), lambda r, i, p: (p[1, r] * (64 // step) + i, 0, 0)),
                    pl.BlockSpec((1, step, spec, 128), lambda r, i, p: (p[0, r], i, 0, 0)),
                ],
                out_specs=pl.BlockSpec((1, sig, step, 2 * sig), lambda r, i, p: (r, 0, i, 0)),
                scratch_shapes=[pltpu.VMEM((sig * step, 128), F32)],
            ),
        )(pick, own, slots)

    in_specs = (P("grp", None, "chan"), P())
    out_specs = P(None, "grp", "chan", None)
    return jax.shard_map(local, mesh=mesh, in_specs=in_specs, out_specs=out_specs, check_vma=False)
```

```python
import functools
import math

import jax
import jax.numpy as jnp
import numpy as np
from jax import lax
from jax.experimental import pallas as pl
from jax.experimental.pallas import tpu as pltpu
from jax.sharding import PartitionSpec as P

TAPS = 16
MESH = pl.DeviceIdType.MESH
F32 = jnp.float32
BF16 = jnp.bfloat16


def coeff_table(fft_len, n_chan):
    position = np.arange(TAPS * fft_len, dtype=np.float64)
    length = TAPS * fft_len
    window = 0.5 - 0.5 * np.cos(2.0 * np.pi * position / length)
    coeff = window * np.sinc((position - 0.5 * length) / fft_len)
    block = fft_len // n_chan
    table = coeff.reshape(TAPS, n_chan, block).transpose(1, 0, 2)
    return np.ascontiguousarray(table.astype(np.float32))


def twiddle_table(fft_len, n_chan):
    block = fft_len // n_chan
    c = np.arange(n_chan // 2 + 1)[:, None]
    m = np.arange(block)[None, :]
    angle = 2.0 * np.pi * (c * m) / fft_len
    return np.stack([np.cos(angle), np.sin(angle)], 1).astype(np.float32)


def second_matrix(fft_len, block):
    half = block // 4
    m = np.arange(block)[:, None]
    j = np.arange(block // 2)[None, :]
    theta = 2.0 * np.pi * (m * j % block) / block
    phi = 2.0 * np.pi * (m * (j + 1) % block) / block
    re = np.concatenate([np.cos(theta), np.sin(theta)], 0)
    im = np.concatenate([-np.sin(theta), np.cos(theta)], 0)
    re_mirror = np.concatenate([np.cos(phi), -np.sin(phi)], 0)
    im_mirror = np.concatenate([-np.sin(phi), -np.cos(phi)], 0)
    parts = []
    for real, imag in ((re, im), (re_mirror, im_mirror)):
        for lo in (0, half):
            parts.append(real[:, lo : lo + half])
            parts.append(imag[:, lo : lo + half])
    full = np.concatenate(parts, 1) / (64.0 * math.sqrt(fft_len))
    high = full.astype(np.float32).astype(BF16)
    low = (full - high.astype(np.float64)).astype(np.float32).astype(BF16)
    return high, low


def real_dft(x):
    n = len(x)
    if n == 1:
        return [(x[0], None)]
    if n == 2:
        return [(x[0] + x[1], None), (x[0] - x[1], None)]
    even = real_dft(x[0::2])
    odd = real_dft(x[1::2])
    out = [None] * (n // 2 + 1)
    out[0] = (even[0][0] + odd[0][0], None)
    out[n // 2] = (even[0][0] - odd[0][0], None)
    quarter = n // 4
    out[quarter] = (even[quarter][0], -odd[quarter][0])
    for c in range(1, quarter):
        er, ei = even[c]
        orr, oi = odd[c]
        angle = 2.0 * math.pi * c / n
        wr, wi = math.cos(angle), -math.sin(angle)
        if 8 * c == n:
            tr, ti = (orr + oi) * wr, (oi - orr) * wr
        else:
            tr, ti = orr * wr - oi * wi, orr * wi + oi * wr
        out[c] = (er + tr, ei + ti)
        out[n // 2 - c] = (er - tr, ti - ei)
    return out


def exchange_kernel(
    dims,
    v_ref, coeff_ref, tw_ref, bh_ref, bl_ref,
    left_ref, slots_ref,
    volts, vf, coeff, tw, bh, bl, filt, r1, zh, zl, s2, r2, r2x, t32, t32x, tn, tx, left,
    load_sem, send1, recv1, send2, recv2, send2x, recv2x, keep_sem, sendq, recvq, relay_sem,
):
    n_chan, plane, sig, spec, block, chunks = dims
    part = spec // chunks
    quarters = n_chan // part
    rows = sig // quarters
    me = lax.axis_index("chan")
    gid = lax.axis_index("grp")
    other = lax.rem(gid + plane, 2 * plane)
    y_hi = gid // plane
    x = lax.rem(gid, plane) // 2
    core = lax.rem(gid, 2)
    n_x = plane // 2
    sib = y_hi * plane + x * 2 + (1 - core)
    loads = [
        pltpu.make_async_copy(v_ref, volts, load_sem.at[0]),
        pltpu.make_async_copy(coeff_ref.at[me], coeff, load_sem.at[1]),
        pltpu.make_async_copy(tw_ref, tw, load_sem.at[2]),
        pltpu.make_async_copy(bh_ref, bh, load_sem.at[3]),
        pltpu.make_async_copy(bl_ref, bl, load_sem.at[4]),
    ]
    for item in loads:
        item.start()
    barrier = pltpu.get_barrier_semaphore()

    def greet(k, carry):
        peer = lax.rem(me + k, n_chan)

        @pl.when(k > 0)
        def _():
            pl.semaphore_signal(barrier, inc=1, device_id={"chan": peer}, device_id_type=MESH)

        pl.semaphore_signal(
            barrier, inc=1, device_id={"grp": other, "chan": peer}, device_id_type=MESH
        )
        return carry

    lax.fori_loop(0, n_chan, greet, 0)
    for dx in range(1, n_x):
        dest = y_hi * plane + lax.rem(x + dx, n_x) * 2 + core
        pl.semaphore_signal(barrier, inc=1, device_id={"grp": dest}, device_id_type=MESH)
    pl.semaphore_signal(barrier, inc=1, device_id={"grp": sib}, device_id_type=MESH)

    loads[1].wait()
    loads[0].wait()

    def widen(lo, hi):
        def body(t, carry):
            vf[t] = volts[t].astype(F32)
            return carry

        lax.fori_loop(lo, hi, body, 0)

    def peer_of(k):
        step = lax.rem(k, 8)
        hop = (step // 2 + 1) * (1 - 2 * lax.rem(step, 2)) * (1 - step // 7)
        z = lax.rem(lax.rem(me, 8) + hop + 8, 8)
        y = lax.rem(me // 8 + k + k // 8, n_chan // 8)
        return y * 8 + z

    def fir(chunk):
        def body(s, carry):
            for lane in range(0, block, 128):
                lanes = pl.ds(lane, 128)
                total = None
                for t in range(TAPS):
                    term = coeff[t : t + 1, lanes] * vf[chunk * part + s + t, :, lanes]
                    total = term if total is None else total + term
                for q in range(quarters):
                    filt[chunk, quarters * s + q, :, lanes] = total[q * rows : (q + 1) * rows].astype(BF16)
            return carry

        lax.fori_loop(0, part, body, 0)

    def copy1(chunk, src, dest):
        return pltpu.make_async_remote_copy(
            src_ref=filt.at[chunk, dest], dst_ref=r1.at[chunk, src],
            send_sem=send1.at[chunk, dest], recv_sem=recv1.at[chunk, src],
            device_id={"chan": dest}, device_id_type=MESH,
        )

    def start1(chunk):
        def body(k, carry):
            dest = peer_of(k)

            @pl.when(dest != me)
            def _():
                copy1(chunk, me, dest).start()

            return carry

        lax.fori_loop(0, n_chan, body, 0)
        pltpu.make_async_copy(filt.at[chunk, me], r1.at[chunk, me], recv1.at[chunk, me]).start()

    widen(0, part + TAPS - 1)
    fir(0)
    pl.semaphore_wait(barrier, 2 * n_chan - 1 + n_x)
    start1(0)
    for chunk in range(1, chunks):
        widen(chunk * part + TAPS - 1, (chunk + 1) * part + TAPS - 1)
        fir(chunk)
        start1(chunk)

    n_half = n_chan // 2

    def copy2(chunk, src, dest):
        return pltpu.make_async_remote_copy(
            src_ref=s2.at[chunk, dest], dst_ref=r2.at[chunk, src],
            send_sem=send2.at[chunk, dest], recv_sem=recv2.at[chunk, src],
            device_id={"chan": dest}, device_id_type=MESH,
        )

    def copy2x(chunk, src, dest):
        return pltpu.make_async_remote_copy(
            src_ref=s2.at[chunk, dest, 1 - y_hi], dst_ref=r2x.at[chunk, src],
            send_sem=send2x.at[chunk, dest], recv_sem=recv2x.at[chunk, src],
            device_id={"grp": other, "chan": dest}, device_id_type=MESH,
        )

    for item in loads[2:]:
        item.wait()

    for chunk in range(chunks):
        def wait1(d, carry):
            pltpu.make_async_copy(r1.at[chunk, d], r1.at[chunk, d], recv1.at[chunk, d]).wait()
            return carry

        lax.fori_loop(0, n_chan, wait1, 0)

        def first(p, carry):
            lane = pl.multiple_of(p * 128, 128)
            samples = [r1[chunk, d, :, pl.ds(lane, 128)].astype(F32) for d in range(n_chan)]
            for c, (re, im) in enumerate(real_dft(samples)):
                cos = tw[c, 0:1, pl.ds(lane, 128)]
                sin = tw[c, 1:2, pl.ds(lane, 128)]
                if im is None:
                    zr, zi = re * cos, -(re * sin)
                else:
                    zr, zi = re * cos + im * sin, im * cos - re * sin
                for base, z in ((0, zr), (block, zi)):
                    lanes = pl.ds(pl.multiple_of(base + lane, 128), 128)
                    high = z.astype(BF16)
                    zh[c, :, lanes] = high
                    zl[c, :, lanes] = (z - high.astype(F32)).astype(BF16)
            return carry

        lax.fori_loop(0, block // 128, first, 0)
        count = (n_half + 1) * rows
        left_h = zh[...].reshape(count, 2 * block)
        left_l = zl[...].reshape(count, 2 * block)
        out = jnp.dot(left_h, bh[...], preferred_element_type=F32)
        out += jnp.dot(left_h, bl[...], preferred_element_type=F32)
        out += jnp.dot(left_l, bh[...], preferred_element_type=F32)
        for c in range(n_half + 1):
            piece = out[c * rows : (c + 1) * rows].astype(BF16)
            s2[chunk, c, 0] = piece[:, 0:128]
            s2[chunk, c, 1] = piece[:, 128:256]
            if 0 < c < n_half:
                s2[chunk, n_chan - c, 0] = piece[:, 256:384]
                s2[chunk, n_chan - c, 1] = piece[:, 384:512]

        def start2x(k, carry):
            copy2x(chunk, me, peer_of(k)).start()
            return carry

        def start2(k, carry):
            dest = peer_of(k)

            @pl.when(dest != me)
            def _():
                copy2(chunk, me, dest).start()

            return carry

        lax.fori_loop(0, n_chan, start2x, 0)
        lax.fori_loop(0, n_chan, start2, 0)
        pltpu.make_async_copy(s2.at[chunk, me], r2.at[chunk, me], recv2.at[chunk, me]).start()

    low_lane = lax.broadcasted_iota(jnp.int32, (sig, 128), 1) < 64

    def swap(a, b):
        re = jnp.where(low_lane, a, pltpu.roll(b, 64, 1))
        im = jnp.where(low_lane, pltpu.roll(a, 64, 1), b)
        return jnp.concatenate([re, im], 0).T

    def copyq(src_ref, chunk, slot, sem, dest_grp):
        return pltpu.make_async_remote_copy(
            src_ref=src_ref, dst_ref=slots_ref.at[slot, chunk], send_sem=sem, recv_sem=recvq.at[chunk, slot],
            device_id={"grp": dest_grp}, device_id_type=MESH,
        )

    half_rows = 64 * part
    sends = []
    relays = []

    def own_blocks(chunk):
        def turn(s, carry):
            for q in range(quarters):
                e = quarters * s + q
                pltpu.make_async_copy(r2.at[chunk, e], r2.at[chunk, e], recv2.at[chunk, e]).wait()
            low = r2[chunk, pl.ds(quarters * s, quarters), 0].reshape(sig, 128).astype(F32)
            high = r2[chunk, pl.ds(quarters * s, quarters), 1].reshape(sig, 128).astype(F32)
            t32[chunk, pl.ds(s, 128, stride=part), :] = swap(low, high)
            return carry

        lax.fori_loop(0, part, turn, 0)

        def pack(i, carry):
            at = pl.ds(pl.multiple_of(i * 128, 128), 128)
            tn[chunk, at] = t32[chunk, at, :].astype(BF16)
            return carry

        lax.fori_loop(0, 2 * half_rows // 128, pack, 0)
        for dx in range(1, n_x):
            dest_x = lax.rem(x + dx, n_x)
            dest = y_hi * plane + dest_x * 2 + core
            upper = (dest_x > x).astype(jnp.int32)
            sends.append(copyq(
                tn.at[chunk, pl.ds(pl.multiple_of(upper * half_rows, half_rows), half_rows)],
                chunk, gid, sendq.at[chunk, dx - 1], dest,
            ))
            sends[-1].start()
        sends.append(copyq(
            tn.at[chunk, pl.ds(pl.multiple_of((1 - core) * half_rows, half_rows), half_rows)],
            chunk, gid, sendq.at[chunk, n_x - 1], sib,
        ))
        sends[-1].start()

    def cross_blocks(chunk):
        def turnx(i, carry):
            for q in range(2 * quarters):
                e = 2 * quarters * i + q
                pltpu.make_async_copy(r2x.at[chunk, e], r2x.at[chunk, e], recv2x.at[chunk, e]).wait()
            first_s = r2x[chunk, pl.ds(2 * quarters * i, quarters)].reshape(sig, 128).astype(F32)
            second_s = r2x[chunk, pl.ds(2 * quarters * i + quarters, quarters)].reshape(sig, 128).astype(F32)
            both = swap(first_s, second_s)
            t32x[pl.ds(2 * i, 64, stride=part), :] = both[:64]
            t32x[pl.ds(2 * i + 1, 64, stride=part), :] = both[64:]
            return carry

        lax.fori_loop(0, part // 2, turnx, 0)

        def packx(i, carry):
            at = pl.ds(pl.multiple_of(i * 128, 128), 128)
            tx[chunk, at] = t32x[at, :].astype(BF16)
            return carry

        lax.fori_loop(0, half_rows // 128, packx, 0)
        for dx in range(1, n_x):
            dest = y_hi * plane + lax.rem(x + dx, n_x) * 2 + core
            sends.append(copyq(tx.at[chunk], chunk, other, sendq.at[chunk, n_x + dx - 1], dest))
            sends[-1].start()
        sends.append(copyq(tx.at[chunk], chunk, other, sendq.at[chunk, 2 * n_x - 1], sib))
        sends[-1].start()
        pltpu.make_async_copy(tx.at[chunk], slots_ref.at[other, chunk], recvq.at[chunk, other]).start()

    def relay(chunk, side):
        for dx in (1, 3, 2):
            source = lax.rem(y_hi + side, 2) * plane + lax.rem(x + n_x - dx, n_x) * 2 + core
            copyq(tx.at[chunk], chunk, source, keep_sem, sib).wait_recv()
            relays.append(copyq(
                slots_ref.at[source, chunk], chunk, source,
                relay_sem.at[chunk, side * (n_x - 1) + dx - 1], sib,
            ))
            relays[-1].start()

    for chunk in range(chunks):
        cross_blocks(chunk)
        if chunk > 0:
            relay(chunk - 1, 1)
        own_blocks(chunk)
        if chunk > 0:
            relay(chunk - 1, 0)

    per = 8 * part

    def prepare(b, carry):
        at = pl.ds(pl.multiple_of(b * per, per), per)
        both = jnp.concatenate([t32[chunk, at, :] for chunk in range(chunks)], 0).T.astype(BF16)
        left[b, :, 0:128] = both[:64]
        left[b, :, 128:256] = both[64:]
        return carry

    lax.fori_loop(0, 16, prepare, 0)
    keep = pltpu.make_async_copy(left, left_ref, keep_sem)
    keep.start()

    relay(chunks - 1, 1)
    relay(chunks - 1, 0)
    for chunk in range(chunks):
        for side in range(2):
            for dx in range(n_x):
                slot = lax.rem(y_hi + side, 2) * plane + lax.rem(x + dx, n_x) * 2 + (1 - core)
                copyq(tx.at[chunk], chunk, slot, keep_sem, sib).wait_recv()
        pltpu.make_async_copy(tx.at[chunk], slots_ref.at[other, chunk], recvq.at[chunk, other]).wait()
    keep.wait()
    for item in sends + relays:
        item.wait_send()

    for chunk in range(chunks):
        def drain(k, carry):
            dest = lax.rem(me + k, n_chan)

            @pl.when(k > 0)
            def _():
                copy1(chunk, me, dest).wait_send()
                copy2(chunk, me, dest).wait_send()

            copy2x(chunk, me, dest).wait_send()
            return carry

        lax.fori_loop(0, n_chan, drain, 0)


def correlate_kernel(
    chunks, spec, plan_ref, left_ref, slots_ref, out_ref, mine, theirs, out, wide, left, left_sem, slot_sem, out_sem
):
    rounds = out.shape[0]
    part = spec // chunks
    per = 8 * part
    gid = lax.axis_index("grp")
    load = pltpu.make_async_copy(left_ref, mine, left_sem)
    load.start()
    fetches = []
    for r in range(rounds):
        fetches.append(pltpu.make_async_copy(slots_ref.at[plan_ref[r, gid]], theirs.at[r], slot_sem.at[r]))
        fetches[-1].start()
    lane_j = lax.rem(lax.broadcasted_iota(jnp.int32, (8, 128), 1), per) // part
    mask = lane_j == lax.broadcasted_iota(jnp.int32, (8, 128), 0)
    low_lane = lax.broadcasted_iota(jnp.int32, (128, 128), 1) < 64
    load.wait()

    def store(r, i):
        at = pl.ds(pl.multiple_of(i * 16, 16), 16)
        return pltpu.make_async_copy(out.at[r, :, at], out_ref.at[r, :, at], out_sem.at[r, i])

    for r in range(rounds):
        fetches[r].wait()
        base = (gid > plan_ref[r, gid]).astype(jnp.int32) * 8

        def step(i, carry):
            results = []
            for b in range(2):
                wide[b] = mine[base + 2 * i + b].astype(F32)
                for a in range(0, 64, 2):
                    for lane in (0, 128):
                        pair = [
                            jnp.where(mask, jnp.broadcast_to(wide[b, a + k : a + k + 1, lane : lane + 128], (8, 128)), 0.0)
                            for k in range(2)
                        ]
                        left[b, 8 * a : 8 * a + 16, lane : lane + 128] = jnp.concatenate(pair, 0).astype(BF16)
                at = pl.ds(pl.multiple_of((2 * i + b) * per, per), per)
                stack = jnp.concatenate([theirs[r, c, at, :] for c in range(chunks)], 0).astype(F32) * (1.0 / spec)
                right = jnp.concatenate(
                    [jnp.where(low_lane, stack, -stack), pltpu.roll(stack, 64, 1)], 0
                ).astype(BF16)
                product = jnp.dot(left[b], right, preferred_element_type=F32)
                results.append(product.reshape(64, 8, 128))
            out[r, :, pl.ds(pl.multiple_of(i * 16, 16), 16), :] = jnp.concatenate(results, 1).astype(BF16)
            store(r, i).start()
            return carry

        lax.fori_loop(0, 4, step, 0)
    for r in range(rounds):
        for i in range(4):
            store(r, i).wait()


def solution(mesh):
    n_chan = mesh.shape["chan"]
    n_grp = mesh.shape["grp"]
    plane = n_grp // 2
    n_x = plane // 2
    chunks = 2

    def local(voltages, plan):
        sig, frames, block = voltages.shape
        spec = frames - TAPS + 1
        part = spec // chunks
        fft_len = block * n_chan
        rows = sig * part // n_chan
        n_c = n_chan // 2 + 1
        rounds = plan.shape[0]
        table = jnp.asarray(coeff_table(fft_len, n_chan))
        twiddle = jnp.asarray(twiddle_table(fft_len, n_chan))
        high, low = second_matrix(fft_len, block)
        anyspace = pl.BlockSpec(memory_space=pl.ANY)
        dma = pltpu.SemaphoreType.DMA
        left, slots = pl.pallas_call(
            functools.partial(exchange_kernel, (n_chan, plane, sig, spec, block, chunks)),
            out_shape=(
                jax.ShapeDtypeStruct((16, 64, 256), BF16),
                jax.ShapeDtypeStruct((n_grp, chunks, 64 * part, 128), BF16),
            ),
            in_specs=[anyspace] * 5,
            out_specs=(anyspace, anyspace),
            scratch_shapes=[
                pltpu.VMEM((frames, sig, block), jnp.int32),
                pltpu.VMEM((frames, sig, block), F32),
                pltpu.VMEM((TAPS, block), F32),
                pltpu.VMEM((n_c, 2, block), F32),
                pltpu.VMEM((2 * block, 2 * block), BF16),
                pltpu.VMEM((2 * block, 2 * block), BF16),
                pltpu.VMEM((chunks, n_chan, rows, block), BF16),
                pltpu.VMEM((chunks, n_chan, rows, block), BF16),
                pltpu.VMEM((n_c, rows, 2 * block), BF16),
                pltpu.VMEM((n_c, rows, 2 * block), BF16),
                pltpu.VMEM((chunks, n_chan, 2, rows, 128), BF16),
                pltpu.VMEM((chunks, n_chan, 2, rows, 128), BF16),
                pltpu.VMEM((chunks, n_chan, rows, 128), BF16),
                pltpu.VMEM((chunks, 128 * part, 128), F32),
                pltpu.VMEM((64 * part, 128), F32),
                pltpu.VMEM((chunks, 128 * part, 128), BF16),
                pltpu.VMEM((chunks, 64 * part, 128), BF16),
                pltpu.VMEM((16, 64, 256), BF16),
                dma((5,)),
                dma((chunks, n_chan)), dma((chunks, n_chan)), dma((chunks, n_chan)),
                dma((chunks, n_chan)), dma((chunks, n_chan)), dma((chunks, n_chan)),
                dma, dma((chunks, 2 * n_x)), dma((chunks, n_grp)), dma((chunks, 2 * n_x)),
            ],
            compiler_params=pltpu.CompilerParams(
                collective_id=0, has_side_effects=True, vmem_limit_bytes=56 * 1024 * 1024
            ),
            cost_estimate=pl.CostEstimate(
                flops=10**9, bytes_accessed=10**7, transcendentals=0
            ),
        )(voltages.transpose(1, 0, 2), table, twiddle, jnp.asarray(high), jnp.asarray(low))
        return pl.pallas_call(
            functools.partial(correlate_kernel, chunks, spec),
            out_shape=jax.ShapeDtypeStruct((rounds, sig, 64, 2 * sig), BF16),
            in_specs=[pl.BlockSpec(memory_space=pltpu.SMEM), anyspace, anyspace],
            out_specs=anyspace,
            scratch_shapes=[
                pltpu.VMEM((16, 64, 256), BF16),
                pltpu.VMEM((rounds, chunks, 64 * part, 128), BF16),
                pltpu.VMEM((rounds, sig, 64, 128), BF16),
                pltpu.VMEM((2, 64, 256), F32),
                pltpu.VMEM((2, 512, 256), BF16),
                dma, dma((rounds,)), dma((rounds, 4)),
            ],
            compiler_params=pltpu.CompilerParams(vmem_limit_bytes=60 * 1024 * 1024),
        )(plan, left, slots)

    in_specs = (P("grp", None, "chan"), P())
    out_specs = P(None, "grp", "chan", None)
    return jax.shard_map(local, mesh=mesh, in_specs=in_specs, out_specs=out_specs, check_vma=False)
```

```python
import functools
import math

import jax
import jax.numpy as jnp
import numpy as np
from jax import lax
from jax.experimental import pallas as pl
from jax.experimental.pallas import tpu as pltpu
from jax.sharding import PartitionSpec as P

TAPS = 16
MESH = pl.DeviceIdType.MESH
F32 = jnp.float32
BF16 = jnp.bfloat16


def coeff_table(fft_len, n_chan):
    position = np.arange(TAPS * fft_len, dtype=np.float64)
    length = TAPS * fft_len
    window = 0.5 - 0.5 * np.cos(2.0 * np.pi * position / length)
    coeff = window * np.sinc((position - 0.5 * length) / fft_len)
    block = fft_len // n_chan
    table = coeff.reshape(TAPS, n_chan, block).transpose(1, 0, 2)
    return np.ascontiguousarray(table.astype(np.float32))


def twiddle_table(fft_len, n_chan):
    block = fft_len // n_chan
    c = np.arange(n_chan // 2 + 1)[:, None]
    m = np.arange(block)[None, :]
    angle = 2.0 * np.pi * (c * m) / fft_len
    return np.stack([np.cos(angle), np.sin(angle)], 1).astype(np.float32)


def second_matrix(fft_len, block):
    half = block // 4
    m = np.arange(block)[:, None]
    j = np.arange(block // 2)[None, :]
    theta = 2.0 * np.pi * (m * j % block) / block
    phi = 2.0 * np.pi * (m * (j + 1) % block) / block
    re = np.concatenate([np.cos(theta), np.sin(theta)], 0)
    im = np.concatenate([-np.sin(theta), np.cos(theta)], 0)
    re_mirror = np.concatenate([np.cos(phi), -np.sin(phi)], 0)
    im_mirror = np.concatenate([-np.sin(phi), -np.cos(phi)], 0)
    parts = []
    for real, imag in ((re, im), (re_mirror, im_mirror)):
        for lo in (0, half):
            parts.append(real[:, lo : lo + half])
            parts.append(imag[:, lo : lo + half])
    full = np.concatenate(parts, 1) / (64.0 * math.sqrt(fft_len))
    high = full.astype(np.float32).astype(BF16)
    low = (full - high.astype(np.float64)).astype(np.float32).astype(BF16)
    return high, low


def real_dft(x):
    n = len(x)
    if n == 1:
        return [(x[0], None)]
    if n == 2:
        return [(x[0] + x[1], None), (x[0] - x[1], None)]
    even = real_dft(x[0::2])
    odd = real_dft(x[1::2])
    out = [None] * (n // 2 + 1)
    out[0] = (even[0][0] + odd[0][0], None)
    out[n // 2] = (even[0][0] - odd[0][0], None)
    quarter = n // 4
    out[quarter] = (even[quarter][0], -odd[quarter][0])
    for c in range(1, quarter):
        er, ei = even[c]
        orr, oi = odd[c]
        angle = 2.0 * math.pi * c / n
        wr, wi = math.cos(angle), -math.sin(angle)
        if 8 * c == n:
            tr, ti = (orr + oi) * wr, (oi - orr) * wr
        else:
            tr, ti = orr * wr - oi * wi, orr * wi + oi * wr
        out[c] = (er + tr, ei + ti)
        out[n // 2 - c] = (er - tr, ti - ei)
    return out


def exchange_kernel(
    dims,
    v_ref, coeff_ref, tw_ref, bh_ref, bl_ref,
    left_ref, slots_ref,
    volts, vf, coeff, tw, bh, bl, filt, r1, zh, zl, s2, r2, r2x, t32, t32x, tn, tx, left,
    load_sem, send1, recv1, send2, recv2, send2x, recv2x, keep_sem, sendq, recvq, relay_sem,
):
    n_chan, plane, sig, spec, block, chunks = dims
    part = spec // chunks
    quarters = n_chan // part
    rows = sig // quarters
    me = lax.axis_index("chan")
    gid = lax.axis_index("grp")
    other = lax.rem(gid + plane, 2 * plane)
    y_hi = gid // plane
    x = lax.rem(gid, plane) // 2
    core = lax.rem(gid, 2)
    n_x = plane // 2
    sib = y_hi * plane + x * 2 + (1 - core)
    loads = [
        pltpu.make_async_copy(v_ref, volts, load_sem.at[0]),
        pltpu.make_async_copy(coeff_ref.at[me], coeff, load_sem.at[1]),
        pltpu.make_async_copy(tw_ref, tw, load_sem.at[2]),
        pltpu.make_async_copy(bh_ref, bh, load_sem.at[3]),
        pltpu.make_async_copy(bl_ref, bl, load_sem.at[4]),
    ]
    for item in loads:
        item.start()
    barrier = pltpu.get_barrier_semaphore()

    def greet(k, carry):
        peer = lax.rem(me + k, n_chan)

        @pl.when(k > 0)
        def _():
            pl.semaphore_signal(barrier, inc=1, device_id={"chan": peer}, device_id_type=MESH)

        pl.semaphore_signal(
            barrier, inc=1, device_id={"grp": other, "chan": peer}, device_id_type=MESH
        )
        return carry

    lax.fori_loop(0, n_chan, greet, 0)
    for dx in range(1, n_x):
        dest = y_hi * plane + lax.rem(x + dx, n_x) * 2 + core
        pl.semaphore_signal(barrier, inc=1, device_id={"grp": dest}, device_id_type=MESH)
    pl.semaphore_signal(barrier, inc=1, device_id={"grp": sib}, device_id_type=MESH)

    loads[1].wait()
    loads[0].wait()

    def widen(lo, hi):
        def body(t, carry):
            vf[t] = volts[t].astype(F32)
            return carry

        lax.fori_loop(lo, hi, body, 0)

    def peer_of(k):
        step = lax.rem(k, 8)
        hop = (step // 2 + 1) * (1 - 2 * lax.rem(step, 2)) * (1 - step // 7)
        z = lax.rem(lax.rem(me, 8) + hop + 8, 8)
        y = lax.rem(me // 8 + k + k // 8, n_chan // 8)
        return y * 8 + z

    def peer_from(k):
        step = lax.rem(k, 8)
        hop = (step // 2 + 1) * (1 - 2 * lax.rem(step, 2)) * (1 - step // 7)
        z = lax.rem(lax.rem(me, 8) - hop + 8, 8)
        y = lax.rem(me // 8 - lax.rem(k + k // 8, n_chan // 8) + n_chan // 8, n_chan // 8)
        return y * 8 + z

    def fir(chunk):
        def body(s, carry):
            for lane in range(0, block, 128):
                lanes = pl.ds(lane, 128)
                total = None
                for t in range(TAPS):
                    term = coeff[t : t + 1, lanes] * vf[chunk * part + s + t, :, lanes]
                    total = term if total is None else total + term
                for q in range(quarters):
                    filt[chunk, quarters * s + q, :, lanes] = total[q * rows : (q + 1) * rows].astype(BF16)
            return carry

        lax.fori_loop(0, part, body, 0)

    def copy1(chunk, src, dest):
        return pltpu.make_async_remote_copy(
            src_ref=filt.at[chunk, dest], dst_ref=r1.at[chunk, src],
            send_sem=send1.at[chunk, dest], recv_sem=recv1.at[chunk, src],
            device_id={"chan": dest}, device_id_type=MESH,
        )

    def start1(chunk):
        def body(k, carry):
            dest = peer_of(k)

            @pl.when(dest != me)
            def _():
                copy1(chunk, me, dest).start()

            return carry

        lax.fori_loop(0, n_chan, body, 0)
        pltpu.make_async_copy(filt.at[chunk, me], r1.at[chunk, me], recv1.at[chunk, me]).start()

    widen(0, part + TAPS - 1)
    def wait1(chunk, lo, hi):
        def body(k, carry):
            d = peer_from(k)
            pltpu.make_async_copy(r1.at[chunk, d], r1.at[chunk, d], recv1.at[chunk, d]).wait()
            return carry

        lax.fori_loop(lo, hi, body, 0)

    widen(0, part + TAPS - 1)
    fir(0)
    pl.semaphore_wait(barrier, 2 * n_chan - 1 + n_x)
    start1(0)
    widen(part + TAPS - 1, spec + TAPS - 1)
    fir(1)
    for item in loads[2:]:
        item.wait()
    start1(1)
    wait1(0, 0, n_chan)

    n_half = n_chan // 2

    def copy2(chunk, src, dest):
        return pltpu.make_async_remote_copy(
            src_ref=s2.at[chunk, dest], dst_ref=r2.at[chunk, src],
            send_sem=send2.at[chunk, dest], recv_sem=recv2.at[chunk, src],
            device_id={"chan": dest}, device_id_type=MESH,
        )

    def copy2x(chunk, src, dest):
        return pltpu.make_async_remote_copy(
            src_ref=s2.at[chunk, dest, 1 - y_hi], dst_ref=r2x.at[chunk, src],
            send_sem=send2x.at[chunk, dest], recv_sem=recv2x.at[chunk, src],
            device_id={"grp": other, "chan": dest}, device_id_type=MESH,
        )

    def transform(chunk):
        def first(p, carry):
            lane = pl.multiple_of(p * 128, 128)
            samples = [r1[chunk, d, :, pl.ds(lane, 128)].astype(F32) for d in range(n_chan)]
            for c, (re, im) in enumerate(real_dft(samples)):
                cos = tw[c, 0:1, pl.ds(lane, 128)]
                sin = tw[c, 1:2, pl.ds(lane, 128)]
                if im is None:
                    zr, zi = re * cos, -(re * sin)
                else:
                    zr, zi = re * cos + im * sin, im * cos - re * sin
                for base, z in ((0, zr), (block, zi)):
                    lanes = pl.ds(pl.multiple_of(base + lane, 128), 128)
                    high = z.astype(BF16)
                    zh[c, :, lanes] = high
                    zl[c, :, lanes] = (z - high.astype(F32)).astype(BF16)
            return carry

        lax.fori_loop(0, block // 128, first, 0)
        count = (n_half + 1) * rows
        left_h = zh[...].reshape(count, 2 * block)
        left_l = zl[...].reshape(count, 2 * block)
        out = jnp.dot(left_h, bh[...], preferred_element_type=F32)
        out += jnp.dot(left_h, bl[...], preferred_element_type=F32)
        out += jnp.dot(left_l, bh[...], preferred_element_type=F32)
        for c in range(n_half + 1):
            piece = out[c * rows : (c + 1) * rows].astype(BF16)
            s2[chunk, c, 0] = piece[:, 0:128]
            s2[chunk, c, 1] = piece[:, 128:256]
            if 0 < c < n_half:
                s2[chunk, n_chan - c, 0] = piece[:, 256:384]
                s2[chunk, n_chan - c, 1] = piece[:, 384:512]

    def start2x(chunk):
        def body(k, carry):
            copy2x(chunk, me, peer_of(k)).start()
            return carry

        lax.fori_loop(0, n_chan, body, 0)

    def start2(chunk):
        def body(k, carry):
            dest = peer_of(k)

            @pl.when(dest != me)
            def _():
                copy2(chunk, me, dest).start()

            return carry

        lax.fori_loop(0, n_chan, body, 0)
        pltpu.make_async_copy(s2.at[chunk, me], r2.at[chunk, me], recv2.at[chunk, me]).start()

    low_lane = lax.broadcasted_iota(jnp.int32, (sig, 128), 1) < 64

    def swap(a, b):
        re = jnp.where(low_lane, a, pltpu.roll(b, 64, 1))
        im = jnp.where(low_lane, pltpu.roll(a, 64, 1), b)
        return jnp.concatenate([re, im], 0).T

    def copyq(src_ref, chunk, slot, sem, dest_grp):
        return pltpu.make_async_remote_copy(
            src_ref=src_ref, dst_ref=slots_ref.at[slot, chunk], send_sem=sem, recv_sem=recvq.at[chunk, slot],
            device_id={"grp": dest_grp}, device_id_type=MESH,
        )

    half_rows = 64 * part
    sends = []
    relays = []

    def own_blocks(chunk):
        def turn(s, carry):
            for q in range(quarters):
                e = quarters * s + q
                pltpu.make_async_copy(r2.at[chunk, e], r2.at[chunk, e], recv2.at[chunk, e]).wait()
            low = r2[chunk, pl.ds(quarters * s, quarters), 0].reshape(sig, 128).astype(F32)
            high = r2[chunk, pl.ds(quarters * s, quarters), 1].reshape(sig, 128).astype(F32)
            t32[chunk, pl.ds(s, 128, stride=part), :] = swap(low, high)
            return carry

        lax.fori_loop(0, part, turn, 0)

        def pack(i, carry):
            at = pl.ds(pl.multiple_of(i * 128, 128), 128)
            tn[chunk, at] = t32[chunk, at, :].astype(BF16)
            return carry

        lax.fori_loop(0, 2 * half_rows // 128, pack, 0)
        for dx in range(1, n_x):
            dest_x = lax.rem(x + dx, n_x)
            dest = y_hi * plane + dest_x * 2 + core
            upper = (dest_x > x).astype(jnp.int32)
            sends.append(copyq(
                tn.at[chunk, pl.ds(pl.multiple_of(upper * half_rows, half_rows), half_rows)],
                chunk, gid, sendq.at[chunk, dx - 1], dest,
            ))
            sends[-1].start()
        sends.append(copyq(
            tn.at[chunk, pl.ds(pl.multiple_of((1 - core) * half_rows, half_rows), half_rows)],
            chunk, gid, sendq.at[chunk, n_x - 1], sib,
        ))
        sends[-1].start()

    def cross_blocks(chunk):
        def turnx(i, carry):
            for q in range(2 * quarters):
                e = 2 * quarters * i + q
                pltpu.make_async_copy(r2x.at[chunk, e], r2x.at[chunk, e], recv2x.at[chunk, e]).wait()
            first_s = r2x[chunk, pl.ds(2 * quarters * i, quarters)].reshape(sig, 128).astype(F32)
            second_s = r2x[chunk, pl.ds(2 * quarters * i + quarters, quarters)].reshape(sig, 128).astype(F32)
            both = swap(first_s, second_s)
            t32x[pl.ds(2 * i, 64, stride=part), :] = both[:64]
            t32x[pl.ds(2 * i + 1, 64, stride=part), :] = both[64:]
            return carry

        lax.fori_loop(0, part // 2, turnx, 0)

        def packx(i, carry):
            at = pl.ds(pl.multiple_of(i * 128, 128), 128)
            tx[chunk, at] = t32x[at, :].astype(BF16)
            return carry

        lax.fori_loop(0, half_rows // 128, packx, 0)
        for dx in range(1, n_x):
            dest = y_hi * plane + lax.rem(x + dx, n_x) * 2 + core
            sends.append(copyq(tx.at[chunk], chunk, other, sendq.at[chunk, n_x + dx - 1], dest))
            sends[-1].start()
        sends.append(copyq(tx.at[chunk], chunk, other, sendq.at[chunk, 2 * n_x - 1], sib))
        sends[-1].start()
        pltpu.make_async_copy(tx.at[chunk], slots_ref.at[other, chunk], recvq.at[chunk, other]).start()

    def relay(chunk, side):
        for dx in (1, 3, 2):
            source = lax.rem(y_hi + side, 2) * plane + lax.rem(x + n_x - dx, n_x) * 2 + core
            copyq(tx.at[chunk], chunk, source, keep_sem, sib).wait_recv()
            relays.append(copyq(
                slots_ref.at[source, chunk], chunk, source,
                relay_sem.at[chunk, side * (n_x - 1) + dx - 1], sib,
            ))
            relays[-1].start()

    transform(0)
    start2x(0)
    start2(0)
    wait1(1, 0, n_chan)
    transform(1)
    cross_blocks(0)
    start2x(1)
    own_blocks(0)
    start2(1)
    cross_blocks(1)
    relay(0, 1)
    own_blocks(1)
    relay(0, 0)

    per = 8 * part

    def prepare(b, carry):
        at = pl.ds(pl.multiple_of(b * per, per), per)
        both = jnp.concatenate([t32[chunk, at, :] for chunk in range(chunks)], 0).T.astype(BF16)
        left[b, :, 0:128] = both[:64]
        left[b, :, 128:256] = both[64:]
        return carry

    lax.fori_loop(0, 16, prepare, 0)
    keep = pltpu.make_async_copy(left, left_ref, keep_sem)
    keep.start()

    relay(chunks - 1, 1)
    relay(chunks - 1, 0)
    for chunk in range(chunks):
        for side in range(2):
            for dx in range(n_x):
                slot = lax.rem(y_hi + side, 2) * plane + lax.rem(x + dx, n_x) * 2 + (1 - core)
                copyq(tx.at[chunk], chunk, slot, keep_sem, sib).wait_recv()
        pltpu.make_async_copy(tx.at[chunk], slots_ref.at[other, chunk], recvq.at[chunk, other]).wait()
    keep.wait()
    for item in sends + relays:
        item.wait_send()

    for chunk in range(chunks):
        def drain(k, carry):
            dest = lax.rem(me + k, n_chan)

            @pl.when(k > 0)
            def _():
                copy1(chunk, me, dest).wait_send()
                copy2(chunk, me, dest).wait_send()

            copy2x(chunk, me, dest).wait_send()
            return carry

        lax.fori_loop(0, n_chan, drain, 0)


def correlate_kernel(
    chunks, spec, plan_ref, left_ref, slots_ref, out_ref, mine, theirs, out, wide, left, left_sem, slot_sem, out_sem
):
    rounds = out.shape[0]
    part = spec // chunks
    per = 8 * part
    gid = lax.axis_index("grp")
    load = pltpu.make_async_copy(left_ref, mine, left_sem)
    load.start()
    fetches = []
    for r in range(rounds):
        fetches.append(pltpu.make_async_copy(slots_ref.at[plan_ref[r, gid]], theirs.at[r], slot_sem.at[r]))
        fetches[-1].start()
    lane_j = lax.rem(lax.broadcasted_iota(jnp.int32, (8, 128), 1), per) // part
    mask = lane_j == lax.broadcasted_iota(jnp.int32, (8, 128), 0)
    low_lane = lax.broadcasted_iota(jnp.int32, (128, 128), 1) < 64
    load.wait()

    def store(r, i):
        at = pl.ds(pl.multiple_of(i * 16, 16), 16)
        return pltpu.make_async_copy(out.at[r, :, at], out_ref.at[r, :, at], out_sem.at[r, i])

    for r in range(rounds):
        fetches[r].wait()
        base = (gid > plan_ref[r, gid]).astype(jnp.int32) * 8

        def step(i, carry):
            results = []
            for b in range(2):
                wide[b] = mine[base + 2 * i + b].astype(F32)
                for a in range(0, 64, 2):
                    for lane in (0, 128):
                        pair = [
                            jnp.where(mask, jnp.broadcast_to(wide[b, a + k : a + k + 1, lane : lane + 128], (8, 128)), 0.0)
                            for k in range(2)
                        ]
                        left[b, 8 * a : 8 * a + 16, lane : lane + 128] = jnp.concatenate(pair, 0).astype(BF16)
                at = pl.ds(pl.multiple_of((2 * i + b) * per, per), per)
                stack = jnp.concatenate([theirs[r, c, at, :] for c in range(chunks)], 0).astype(F32) * (1.0 / spec)
                right = jnp.concatenate(
                    [jnp.where(low_lane, stack, -stack), pltpu.roll(stack, 64, 1)], 0
                ).astype(BF16)
                product = jnp.dot(left[b], right, preferred_element_type=F32)
                results.append(product.reshape(64, 8, 128))
            out[r, :, pl.ds(pl.multiple_of(i * 16, 16), 16), :] = jnp.concatenate(results, 1).astype(BF16)
            store(r, i).start()
            return carry

        lax.fori_loop(0, 4, step, 0)
    for r in range(rounds):
        for i in range(4):
            store(r, i).wait()


def solution(mesh):
    n_chan = mesh.shape["chan"]
    n_grp = mesh.shape["grp"]
    plane = n_grp // 2
    n_x = plane // 2
    chunks = 2

    def local(voltages, plan):
        sig, frames, block = voltages.shape
        spec = frames - TAPS + 1
        part = spec // chunks
        fft_len = block * n_chan
        rows = sig * part // n_chan
        n_c = n_chan // 2 + 1
        rounds = plan.shape[0]
        table = jnp.asarray(coeff_table(fft_len, n_chan))
        twiddle = jnp.asarray(twiddle_table(fft_len, n_chan))
        high, low = second_matrix(fft_len, block)
        anyspace = pl.BlockSpec(memory_space=pl.ANY)
        dma = pltpu.SemaphoreType.DMA
        left, slots = pl.pallas_call(
            functools.partial(exchange_kernel, (n_chan, plane, sig, spec, block, chunks)),
            out_shape=(
                jax.ShapeDtypeStruct((16, 64, 256), BF16),
                jax.ShapeDtypeStruct((n_grp, chunks, 64 * part, 128), BF16),
            ),
            in_specs=[anyspace] * 5,
            out_specs=(anyspace, anyspace),
            scratch_shapes=[
                pltpu.VMEM((frames, sig, block), jnp.int32),
                pltpu.VMEM((frames, sig, block), F32),
                pltpu.VMEM((TAPS, block), F32),
                pltpu.VMEM((n_c, 2, block), F32),
                pltpu.VMEM((2 * block, 2 * block), BF16),
                pltpu.VMEM((2 * block, 2 * block), BF16),
                pltpu.VMEM((chunks, n_chan, rows, block), BF16),
                pltpu.VMEM((chunks, n_chan, rows, block), BF16),
                pltpu.VMEM((n_c, rows, 2 * block), BF16),
                pltpu.VMEM((n_c, rows, 2 * block), BF16),
                pltpu.VMEM((chunks, n_chan, 2, rows, 128), BF16),
                pltpu.VMEM((chunks, n_chan, 2, rows, 128), BF16),
                pltpu.VMEM((chunks, n_chan, rows, 128), BF16),
                pltpu.VMEM((chunks, 128 * part, 128), F32),
                pltpu.VMEM((64 * part, 128), F32),
                pltpu.VMEM((chunks, 128 * part, 128), BF16),
                pltpu.VMEM((chunks, 64 * part, 128), BF16),
                pltpu.VMEM((16, 64, 256), BF16),
                dma((5,)),
                dma((chunks, n_chan)), dma((chunks, n_chan)), dma((chunks, n_chan)),
                dma((chunks, n_chan)), dma((chunks, n_chan)), dma((chunks, n_chan)),
                dma, dma((chunks, 2 * n_x)), dma((chunks, n_grp)), dma((chunks, 2 * n_x)),
            ],
            compiler_params=pltpu.CompilerParams(
                collective_id=0, has_side_effects=True, vmem_limit_bytes=56 * 1024 * 1024
            ),
            cost_estimate=pl.CostEstimate(
                flops=10**9, bytes_accessed=10**7, transcendentals=0
            ),
        )(voltages.transpose(1, 0, 2), table, twiddle, jnp.asarray(high), jnp.asarray(low))
        return pl.pallas_call(
            functools.partial(correlate_kernel, chunks, spec),
            out_shape=jax.ShapeDtypeStruct((rounds, sig, 64, 2 * sig), BF16),
            in_specs=[pl.BlockSpec(memory_space=pltpu.SMEM), anyspace, anyspace],
            out_specs=anyspace,
            scratch_shapes=[
                pltpu.VMEM((16, 64, 256), BF16),
                pltpu.VMEM((rounds, chunks, 64 * part, 128), BF16),
                pltpu.VMEM((rounds, sig, 64, 128), BF16),
                pltpu.VMEM((2, 64, 256), F32),
                pltpu.VMEM((2, 512, 256), BF16),
                dma, dma((rounds,)), dma((rounds, 4)),
            ],
            compiler_params=pltpu.CompilerParams(vmem_limit_bytes=60 * 1024 * 1024),
        )(plan, left, slots)

    in_specs = (P("grp", None, "chan"), P())
    out_specs = P(None, "grp", "chan", None)
    return jax.shard_map(local, mesh=mesh, in_specs=in_specs, out_specs=out_specs, check_vma=False)
```

```python
import functools
import math

import jax
import jax.numpy as jnp
import numpy as np
from jax import lax
from jax.experimental import pallas as pl
from jax.experimental.pallas import tpu as pltpu
from jax.sharding import PartitionSpec as P

TAPS = 16
MESH = pl.DeviceIdType.MESH
F32 = jnp.float32
BF16 = jnp.bfloat16


def coeff_table(fft_len, n_chan):
    position = np.arange(TAPS * fft_len, dtype=np.float64)
    length = TAPS * fft_len
    window = 0.5 - 0.5 * np.cos(2.0 * np.pi * position / length)
    coeff = window * np.sinc((position - 0.5 * length) / fft_len)
    block = fft_len // n_chan
    table = coeff.reshape(TAPS, n_chan, block).transpose(1, 0, 2)
    return np.ascontiguousarray(table.astype(np.float32))


def twiddle_table(fft_len, n_chan):
    block = fft_len // n_chan
    c = np.arange(n_chan // 2 + 1)[:, None]
    m = np.arange(block)[None, :]
    angle = 2.0 * np.pi * (c * m) / fft_len
    return np.stack([np.cos(angle), np.sin(angle)], 1).astype(np.float32)


def second_matrix(fft_len, block):
    half = block // 4
    m = np.arange(block)[:, None]
    j = np.arange(block // 2)[None, :]
    theta = 2.0 * np.pi * (m * j % block) / block
    phi = 2.0 * np.pi * (m * (j + 1) % block) / block
    re = np.concatenate([np.cos(theta), np.sin(theta)], 0)
    im = np.concatenate([-np.sin(theta), np.cos(theta)], 0)
    re_mirror = np.concatenate([np.cos(phi), -np.sin(phi)], 0)
    im_mirror = np.concatenate([-np.sin(phi), -np.cos(phi)], 0)
    parts = []
    for real, imag in ((re, im), (re_mirror, im_mirror)):
        for lo in (0, half):
            parts.append(real[:, lo : lo + half])
            parts.append(imag[:, lo : lo + half])
    full = np.concatenate(parts, 1) / (64.0 * math.sqrt(fft_len))
    high = full.astype(np.float32).astype(BF16)
    low = (full - high.astype(np.float64)).astype(np.float32).astype(BF16)
    return high, low


def real_dft(x):
    n = len(x)
    if n == 1:
        return [(x[0], None)]
    if n == 2:
        return [(x[0] + x[1], None), (x[0] - x[1], None)]
    even = real_dft(x[0::2])
    odd = real_dft(x[1::2])
    out = [None] * (n // 2 + 1)
    out[0] = (even[0][0] + odd[0][0], None)
    out[n // 2] = (even[0][0] - odd[0][0], None)
    quarter = n // 4
    out[quarter] = (even[quarter][0], -odd[quarter][0])
    for c in range(1, quarter):
        er, ei = even[c]
        orr, oi = odd[c]
        angle = 2.0 * math.pi * c / n
        wr, wi = math.cos(angle), -math.sin(angle)
        if 8 * c == n:
            tr, ti = (orr + oi) * wr, (oi - orr) * wr
        else:
            tr, ti = orr * wr - oi * wi, orr * wi + oi * wr
        out[c] = (er + tr, ei + ti)
        out[n // 2 - c] = (er - tr, ti - ei)
    return out


def exchange_kernel(
    dims,
    v_ref, coeff_ref, tw_ref, bh_ref, bl_ref,
    left_ref, slots_ref,
    volts, vf, coeff, tw, bh, bl, filt, r1, zh, zl, s2, r2, r2x, t32, t32x, tn, tx, left,
    load_sem, send1, recv1, send2, recv2, send2x, recv2x, keep_sem, sendq, recvq, relay_sem, row_sem,
):
    n_chan, plane, sig, spec, block, chunks = dims
    part = spec // chunks
    quarters = n_chan // part
    rows = sig // quarters
    me = lax.axis_index("chan")
    gid = lax.axis_index("grp")
    other = lax.rem(gid + plane, 2 * plane)
    y_hi = gid // plane
    x = lax.rem(gid, plane) // 2
    core = lax.rem(gid, 2)
    n_x = plane // 2
    sib = y_hi * plane + x * 2 + (1 - core)
    loads = [
        pltpu.make_async_copy(v_ref, volts, load_sem.at[0]),
        pltpu.make_async_copy(coeff_ref.at[me], coeff, load_sem.at[1]),
        pltpu.make_async_copy(tw_ref, tw, load_sem.at[2]),
        pltpu.make_async_copy(bh_ref, bh, load_sem.at[3]),
        pltpu.make_async_copy(bl_ref, bl, load_sem.at[4]),
    ]
    for item in loads:
        item.start()
    barrier = pltpu.get_barrier_semaphore()

    def greet(k, carry):
        peer = lax.rem(me + k, n_chan)
        pl.semaphore_signal(barrier, inc=1, device_id={"chan": peer}, device_id_type=MESH)
        return carry

    lax.fori_loop(1, n_chan, greet, 0)
    pl.semaphore_signal(barrier, inc=1, device_id={"grp": other}, device_id_type=MESH)
    for dx in range(1, n_x):
        dest = y_hi * plane + lax.rem(x + dx, n_x) * 2 + core
        pl.semaphore_signal(barrier, inc=1, device_id={"grp": dest}, device_id_type=MESH)
    pl.semaphore_signal(barrier, inc=1, device_id={"grp": sib}, device_id_type=MESH)

    loads[1].wait()
    loads[0].wait()

    def widen(lo, hi):
        def body(t, carry):
            vf[t] = volts[t].astype(F32)
            return carry

        lax.fori_loop(lo, hi, body, 0)

    def peer_of(k):
        step = lax.rem(k, 8)
        hop = (step // 2 + 1) * (1 - 2 * lax.rem(step, 2)) * (1 - step // 7)
        z = lax.rem(lax.rem(me, 8) + hop + 8, 8)
        y = lax.rem(me // 8 + k + k // 8, n_chan // 8)
        return y * 8 + z

    def peer_from(k):
        step = lax.rem(k, 8)
        hop = (step // 2 + 1) * (1 - 2 * lax.rem(step, 2)) * (1 - step // 7)
        z = lax.rem(lax.rem(me, 8) - hop + 8, 8)
        y = lax.rem(me // 8 - lax.rem(k + k // 8, n_chan // 8) + n_chan // 8, n_chan // 8)
        return y * 8 + z

    def fir(chunk):
        def body(s, carry):
            for lane in range(0, block, 128):
                lanes = pl.ds(lane, 128)
                total = None
                for t in range(TAPS):
                    term = coeff[t : t + 1, lanes] * vf[chunk * part + s + t, :, lanes]
                    total = term if total is None else total + term
                for q in range(quarters):
                    filt[chunk, quarters * s + q, :, lanes] = total[q * rows : (q + 1) * rows].astype(BF16)
            return carry

        lax.fori_loop(0, part, body, 0)

    def copy1(chunk, src, dest):
        return pltpu.make_async_remote_copy(
            src_ref=filt.at[chunk, dest], dst_ref=r1.at[chunk, src],
            send_sem=send1.at[chunk, dest], recv_sem=recv1.at[chunk, src],
            device_id={"chan": dest}, device_id_type=MESH,
        )

    def start1(chunk):
        def body(k, carry):
            dest = peer_of(k)

            @pl.when(dest != me)
            def _():
                copy1(chunk, me, dest).start()

            return carry

        lax.fori_loop(0, n_chan, body, 0)
        pltpu.make_async_copy(filt.at[chunk, me], r1.at[chunk, me], recv1.at[chunk, me]).start()

    widen(0, part + TAPS - 1)
    def wait1(chunk, lo, hi):
        def body(k, carry):
            d = peer_from(k)
            pltpu.make_async_copy(r1.at[chunk, d], r1.at[chunk, d], recv1.at[chunk, d]).wait()
            return carry

        lax.fori_loop(lo, hi, body, 0)

    widen(0, part + TAPS - 1)
    fir(0)
    pl.semaphore_wait(barrier, n_chan + n_x)
    pl.semaphore_signal(row_sem, inc=1, device_id={"grp": other}, device_id_type=MESH)
    start1(0)
    widen(part + TAPS - 1, spec + TAPS - 1)
    fir(1)
    for item in loads[2:]:
        item.wait()
    start1(1)
    wait1(0, 0, n_chan)

    n_half = n_chan // 2

    def copy2(chunk, src, dest):
        return pltpu.make_async_remote_copy(
            src_ref=s2.at[chunk, dest], dst_ref=r2.at[chunk, src],
            send_sem=send2.at[chunk, dest], recv_sem=recv2.at[chunk, src],
            device_id={"chan": dest}, device_id_type=MESH,
        )

    def copy2x(chunk, src, dest):
        return pltpu.make_async_remote_copy(
            src_ref=s2.at[chunk, dest, 1 - y_hi], dst_ref=r2x.at[chunk, src],
            send_sem=send2x.at[chunk, dest], recv_sem=recv2x.at[chunk, src],
            device_id={"grp": other, "chan": dest}, device_id_type=MESH,
        )

    def transform(chunk):
        def first(p, carry):
            lane = pl.multiple_of(p * 128, 128)
            samples = [r1[chunk, d, :, pl.ds(lane, 128)].astype(F32) for d in range(n_chan)]
            for c, (re, im) in enumerate(real_dft(samples)):
                cos = tw[c, 0:1, pl.ds(lane, 128)]
                sin = tw[c, 1:2, pl.ds(lane, 128)]
                if im is None:
                    zr, zi = re * cos, -(re * sin)
                else:
                    zr, zi = re * cos + im * sin, im * cos - re * sin
                for base, z in ((0, zr), (block, zi)):
                    lanes = pl.ds(pl.multiple_of(base + lane, 128), 128)
                    high = z.astype(BF16)
                    zh[c, :, lanes] = high
                    zl[c, :, lanes] = (z - high.astype(F32)).astype(BF16)
            return carry

        lax.fori_loop(0, block // 128, first, 0)
        count = (n_half + 1) * rows
        left_h = zh[...].reshape(count, 2 * block)
        left_l = zl[...].reshape(count, 2 * block)
        out = jnp.dot(left_h, bh[...], preferred_element_type=F32)
        out += jnp.dot(left_h, bl[...], preferred_element_type=F32)
        out += jnp.dot(left_l, bh[...], preferred_element_type=F32)
        for c in range(n_half + 1):
            piece = out[c * rows : (c + 1) * rows].astype(BF16)
            s2[chunk, c, 0] = piece[:, 0:128]
            s2[chunk, c, 1] = piece[:, 128:256]
            if 0 < c < n_half:
                s2[chunk, n_chan - c, 0] = piece[:, 256:384]
                s2[chunk, n_chan - c, 1] = piece[:, 384:512]

    def start2x(chunk):
        def body(k, carry):
            copy2x(chunk, me, peer_of(k)).start()
            return carry

        lax.fori_loop(0, n_chan, body, 0)

    def start2(chunk):
        def body(k, carry):
            dest = peer_of(k)

            @pl.when(dest != me)
            def _():
                copy2(chunk, me, dest).start()

            return carry

        lax.fori_loop(0, n_chan, body, 0)
        pltpu.make_async_copy(s2.at[chunk, me], r2.at[chunk, me], recv2.at[chunk, me]).start()

    low_lane = lax.broadcasted_iota(jnp.int32, (sig, 128), 1) < 64

    def swap(a, b):
        re = jnp.where(low_lane, a, pltpu.roll(b, 64, 1))
        im = jnp.where(low_lane, pltpu.roll(a, 64, 1), b)
        return jnp.concatenate([re, im], 0).T

    def copyq(src_ref, chunk, slot, sem, dest_grp):
        return pltpu.make_async_remote_copy(
            src_ref=src_ref, dst_ref=slots_ref.at[slot, chunk], send_sem=sem, recv_sem=recvq.at[chunk, slot],
            device_id={"grp": dest_grp}, device_id_type=MESH,
        )

    half_rows = 64 * part
    sends = []
    relays = []

    def own_blocks(chunk):
        def turn(s, carry):
            for q in range(quarters):
                e = quarters * s + q
                pltpu.make_async_copy(r2.at[chunk, e], r2.at[chunk, e], recv2.at[chunk, e]).wait()
            low = r2[chunk, pl.ds(quarters * s, quarters), 0].reshape(sig, 128).astype(F32)
            high = r2[chunk, pl.ds(quarters * s, quarters), 1].reshape(sig, 128).astype(F32)
            t32[chunk, pl.ds(s, 128, stride=part), :] = swap(low, high)
            return carry

        lax.fori_loop(0, part, turn, 0)

        def pack(i, carry):
            at = pl.ds(pl.multiple_of(i * 128, 128), 128)
            tn[chunk, at] = t32[chunk, at, :].astype(BF16)
            return carry

        lax.fori_loop(0, 2 * half_rows // 128, pack, 0)
        for dx in range(1, n_x):
            dest_x = lax.rem(x + dx, n_x)
            dest = y_hi * plane + dest_x * 2 + core
            upper = (dest_x > x).astype(jnp.int32)
            sends.append(copyq(
                tn.at[chunk, pl.ds(pl.multiple_of(upper * half_rows, half_rows), half_rows)],
                chunk, gid, sendq.at[chunk, dx - 1], dest,
            ))
            sends[-1].start()
        sends.append(copyq(
            tn.at[chunk, pl.ds(pl.multiple_of((1 - core) * half_rows, half_rows), half_rows)],
            chunk, gid, sendq.at[chunk, n_x - 1], sib,
        ))
        sends[-1].start()

    def cross_blocks(chunk):
        def turnx(i, carry):
            for q in range(2 * quarters):
                e = 2 * quarters * i + q
                pltpu.make_async_copy(r2x.at[chunk, e], r2x.at[chunk, e], recv2x.at[chunk, e]).wait()
            first_s = r2x[chunk, pl.ds(2 * quarters * i, quarters)].reshape(sig, 128).astype(F32)
            second_s = r2x[chunk, pl.ds(2 * quarters * i + quarters, quarters)].reshape(sig, 128).astype(F32)
            both = swap(first_s, second_s)
            t32x[pl.ds(2 * i, 64, stride=part), :] = both[:64]
            t32x[pl.ds(2 * i + 1, 64, stride=part), :] = both[64:]
            return carry

        lax.fori_loop(0, part // 2, turnx, 0)

        def packx(i, carry):
            at = pl.ds(pl.multiple_of(i * 128, 128), 128)
            tx[chunk, at] = t32x[at, :].astype(BF16)
            return carry

        lax.fori_loop(0, half_rows // 128, packx, 0)
        for dx in range(1, n_x):
            dest = y_hi * plane + lax.rem(x + dx, n_x) * 2 + core
            sends.append(copyq(tx.at[chunk], chunk, other, sendq.at[chunk, n_x + dx - 1], dest))
            sends[-1].start()
        sends.append(copyq(tx.at[chunk], chunk, other, sendq.at[chunk, 2 * n_x - 1], sib))
        sends[-1].start()
        pltpu.make_async_copy(tx.at[chunk], slots_ref.at[other, chunk], recvq.at[chunk, other]).start()

    def relay(chunk, side):
        for dx in (1, 3, 2):
            source = lax.rem(y_hi + side, 2) * plane + lax.rem(x + n_x - dx, n_x) * 2 + core
            copyq(tx.at[chunk], chunk, source, keep_sem, sib).wait_recv()
            relays.append(copyq(
                slots_ref.at[source, chunk], chunk, source,
                relay_sem.at[chunk, side * (n_x - 1) + dx - 1], sib,
            ))
            relays[-1].start()

    transform(0)
    pl.semaphore_wait(row_sem, 1)
    start2x(0)
    start2(0)
    wait1(1, 0, n_chan)
    transform(1)
    cross_blocks(0)
    start2x(1)
    own_blocks(0)
    start2(1)
    cross_blocks(1)
    relay(0, 1)
    own_blocks(1)
    relay(0, 0)

    per = 8 * part

    def prepare(b, carry):
        at = pl.ds(pl.multiple_of(b * per, per), per)
        both = jnp.concatenate([t32[chunk, at, :] for chunk in range(chunks)], 0).T.astype(BF16)
        left[b, :, 0:128] = both[:64]
        left[b, :, 128:256] = both[64:]
        return carry

    lax.fori_loop(0, 16, prepare, 0)
    keep = pltpu.make_async_copy(left, left_ref, keep_sem)
    keep.start()

    relay(chunks - 1, 1)
    relay(chunks - 1, 0)
    for chunk in range(chunks):
        for side in range(2):
            for dx in range(n_x):
                slot = lax.rem(y_hi + side, 2) * plane + lax.rem(x + dx, n_x) * 2 + (1 - core)
                copyq(tx.at[chunk], chunk, slot, keep_sem, sib).wait_recv()
        pltpu.make_async_copy(tx.at[chunk], slots_ref.at[other, chunk], recvq.at[chunk, other]).wait()
    keep.wait()
    for item in sends + relays:
        item.wait_send()

    for chunk in range(chunks):
        def drain(k, carry):
            dest = lax.rem(me + k, n_chan)

            @pl.when(k > 0)
            def _():
                copy1(chunk, me, dest).wait_send()
                copy2(chunk, me, dest).wait_send()

            copy2x(chunk, me, dest).wait_send()
            return carry

        lax.fori_loop(0, n_chan, drain, 0)


def correlate_kernel(
    chunks, spec, plan_ref, left_ref, slots_ref, out_ref, mine, theirs, out, wide, left, left_sem, slot_sem, out_sem
):
    rounds = out.shape[0]
    part = spec // chunks
    per = 8 * part
    gid = lax.axis_index("grp")
    load = pltpu.make_async_copy(left_ref, mine, left_sem)
    load.start()
    fetches = []
    for r in range(rounds):
        fetches.append(pltpu.make_async_copy(slots_ref.at[plan_ref[r, gid]], theirs.at[r], slot_sem.at[r]))
        fetches[-1].start()
    lane_j = lax.rem(lax.broadcasted_iota(jnp.int32, (8, 128), 1), per) // part
    mask = lane_j == lax.broadcasted_iota(jnp.int32, (8, 128), 0)
    low_lane = lax.broadcasted_iota(jnp.int32, (128, 128), 1) < 64
    load.wait()

    def store(r, i):
        at = pl.ds(pl.multiple_of(i * 16, 16), 16)
        return pltpu.make_async_copy(out.at[r, :, at], out_ref.at[r, :, at], out_sem.at[r, i])

    for r in range(rounds):
        fetches[r].wait()

    def step(i, carry):
        for u in range(2):
            for b in range(2):
                wide[...] = mine[u * 8 + 2 * i + b].astype(F32)
                for a in range(0, 64, 2):
                    for lane in (0, 128):
                        pair = [
                            jnp.where(mask, jnp.broadcast_to(wide[a + k : a + k + 1, lane : lane + 128], (8, 128)), 0.0)
                            for k in range(2)
                        ]
                        left[u, b, 8 * a : 8 * a + 16, lane : lane + 128] = jnp.concatenate(pair, 0).astype(BF16)
        for r in range(rounds):
            u = (gid > plan_ref[r, gid]).astype(jnp.int32)
            results = []
            for b in range(2):
                at = pl.ds(pl.multiple_of((2 * i + b) * per, per), per)
                stack = jnp.concatenate([theirs[r, c, at, :] for c in range(chunks)], 0).astype(F32) * (1.0 / spec)
                right = jnp.concatenate(
                    [jnp.where(low_lane, stack, -stack), pltpu.roll(stack, 64, 1)], 0
                ).astype(BF16)
                product = jnp.dot(left[u, b], right, preferred_element_type=F32)
                results.append(product.reshape(64, 8, 128))
            out[r, :, pl.ds(pl.multiple_of(i * 16, 16), 16), :] = jnp.concatenate(results, 1).astype(BF16)
            store(r, i).start()
        return carry

    lax.fori_loop(0, 4, step, 0)
    for r in range(rounds):
        for i in range(4):
            store(r, i).wait()


def solution(mesh):
    n_chan = mesh.shape["chan"]
    n_grp = mesh.shape["grp"]
    plane = n_grp // 2
    n_x = plane // 2
    chunks = 2

    def local(voltages, plan):
        sig, frames, block = voltages.shape
        spec = frames - TAPS + 1
        part = spec // chunks
        fft_len = block * n_chan
        rows = sig * part // n_chan
        n_c = n_chan // 2 + 1
        rounds = plan.shape[0]
        table = jnp.asarray(coeff_table(fft_len, n_chan))
        twiddle = jnp.asarray(twiddle_table(fft_len, n_chan))
        high, low = second_matrix(fft_len, block)
        anyspace = pl.BlockSpec(memory_space=pl.ANY)
        dma = pltpu.SemaphoreType.DMA
        left, slots = pl.pallas_call(
            functools.partial(exchange_kernel, (n_chan, plane, sig, spec, block, chunks)),
            out_shape=(
                jax.ShapeDtypeStruct((16, 64, 256), BF16),
                jax.ShapeDtypeStruct((n_grp, chunks, 64 * part, 128), BF16),
            ),
            in_specs=[anyspace] * 5,
            out_specs=(anyspace, anyspace),
            scratch_shapes=[
                pltpu.VMEM((frames, sig, block), jnp.int32),
                pltpu.VMEM((frames, sig, block), F32),
                pltpu.VMEM((TAPS, block), F32),
                pltpu.VMEM((n_c, 2, block), F32),
                pltpu.VMEM((2 * block, 2 * block), BF16),
                pltpu.VMEM((2 * block, 2 * block), BF16),
                pltpu.VMEM((chunks, n_chan, rows, block), BF16),
                pltpu.VMEM((chunks, n_chan, rows, block), BF16),
                pltpu.VMEM((n_c, rows, 2 * block), BF16),
                pltpu.VMEM((n_c, rows, 2 * block), BF16),
                pltpu.VMEM((chunks, n_chan, 2, rows, 128), BF16),
                pltpu.VMEM((chunks, n_chan, 2, rows, 128), BF16),
                pltpu.VMEM((chunks, n_chan, rows, 128), BF16),
                pltpu.VMEM((chunks, 128 * part, 128), F32),
                pltpu.VMEM((64 * part, 128), F32),
                pltpu.VMEM((chunks, 128 * part, 128), BF16),
                pltpu.VMEM((chunks, 64 * part, 128), BF16),
                pltpu.VMEM((16, 64, 256), BF16),
                dma((5,)),
                dma((chunks, n_chan)), dma((chunks, n_chan)), dma((chunks, n_chan)),
                dma((chunks, n_chan)), dma((chunks, n_chan)), dma((chunks, n_chan)),
                dma, dma((chunks, 2 * n_x)), dma((chunks, n_grp)), dma((chunks, 2 * n_x)),
                pltpu.SemaphoreType.REGULAR,
            ],
            compiler_params=pltpu.CompilerParams(
                collective_id=0, has_side_effects=True, vmem_limit_bytes=56 * 1024 * 1024
            ),
            cost_estimate=pl.CostEstimate(
                flops=10**9, bytes_accessed=10**7, transcendentals=0
            ),
        )(voltages.transpose(1, 0, 2), table, twiddle, jnp.asarray(high), jnp.asarray(low))
        return pl.pallas_call(
            functools.partial(correlate_kernel, chunks, spec),
            out_shape=jax.ShapeDtypeStruct((rounds, sig, 64, 2 * sig), BF16),
            in_specs=[pl.BlockSpec(memory_space=pltpu.SMEM), anyspace, anyspace],
            out_specs=anyspace,
            scratch_shapes=[
                pltpu.VMEM((16, 64, 256), BF16),
                pltpu.VMEM((rounds, chunks, 64 * part, 128), BF16),
                pltpu.VMEM((rounds, sig, 64, 128), BF16),
                pltpu.VMEM((64, 256), F32),
                pltpu.VMEM((2, 2, 512, 256), BF16),
                dma, dma((rounds,)), dma((rounds, 4)),
            ],
            compiler_params=pltpu.CompilerParams(vmem_limit_bytes=60 * 1024 * 1024),
        )(plan, left, slots)

    in_specs = (P("grp", None, "chan"), P())
    out_specs = P(None, "grp", "chan", None)
    return jax.shard_map(local, mesh=mesh, in_specs=in_specs, out_specs=out_specs, check_vma=False)
```

```python
import functools
import math

import jax
import jax.numpy as jnp
import numpy as np
from jax import lax
from jax.experimental import pallas as pl
from jax.experimental.pallas import tpu as pltpu
from jax.sharding import PartitionSpec as P

TAPS = 16
MESH = pl.DeviceIdType.MESH
F32 = jnp.float32
BF16 = jnp.bfloat16


def coeff_table(fft_len, n_chan):
    position = np.arange(TAPS * fft_len, dtype=np.float64)
    length = TAPS * fft_len
    window = 0.5 - 0.5 * np.cos(2.0 * np.pi * position / length)
    coeff = window * np.sinc((position - 0.5 * length) / fft_len)
    block = fft_len // n_chan
    table = coeff.reshape(TAPS, n_chan, block).transpose(1, 0, 2)
    return np.ascontiguousarray(table.astype(np.float32))


def twiddle_table(fft_len, n_chan):
    block = fft_len // n_chan
    c = np.arange(n_chan // 2 + 1)[:, None]
    m = np.arange(block)[None, :]
    angle = 2.0 * np.pi * (c * m) / fft_len
    return np.stack([np.cos(angle), np.sin(angle)], 1).astype(np.float32)


def second_matrix(fft_len, block):
    half = block // 4
    m = np.arange(block)[:, None]
    j = np.arange(block // 2)[None, :]
    theta = 2.0 * np.pi * (m * j % block) / block
    phi = 2.0 * np.pi * (m * (j + 1) % block) / block
    re = np.concatenate([np.cos(theta), np.sin(theta)], 0)
    im = np.concatenate([-np.sin(theta), np.cos(theta)], 0)
    re_mirror = np.concatenate([np.cos(phi), -np.sin(phi)], 0)
    im_mirror = np.concatenate([-np.sin(phi), -np.cos(phi)], 0)
    parts = []
    for real, imag in ((re, im), (re_mirror, im_mirror)):
        for lo in (0, half):
            parts.append(real[:, lo : lo + half])
            parts.append(imag[:, lo : lo + half])
    full = np.concatenate(parts, 1) / (64.0 * math.sqrt(fft_len))
    high = full.astype(np.float32).astype(BF16)
    low = (full - high.astype(np.float64)).astype(np.float32).astype(BF16)
    return high, low


def real_dft(x):
    n = len(x)
    if n == 1:
        return [(x[0], None)]
    if n == 2:
        return [(x[0] + x[1], None), (x[0] - x[1], None)]
    even = real_dft(x[0::2])
    odd = real_dft(x[1::2])
    out = [None] * (n // 2 + 1)
    out[0] = (even[0][0] + odd[0][0], None)
    out[n // 2] = (even[0][0] - odd[0][0], None)
    quarter = n // 4
    out[quarter] = (even[quarter][0], -odd[quarter][0])
    for c in range(1, quarter):
        er, ei = even[c]
        orr, oi = odd[c]
        angle = 2.0 * math.pi * c / n
        wr, wi = math.cos(angle), -math.sin(angle)
        if 8 * c == n:
            tr, ti = (orr + oi) * wr, (oi - orr) * wr
        else:
            tr, ti = orr * wr - oi * wi, orr * wi + oi * wr
        out[c] = (er + tr, ei + ti)
        out[n // 2 - c] = (er - tr, ti - ei)
    return out


def exchange_kernel(
    dims,
    v_ref, coeff_ref, tw_ref, bh_ref, bl_ref,
    left_ref, slots_ref,
    volts, vf, coeff, tw, bh, bl, filt, r1, zh, zl, s2, r2, r2x, t32, t32x, tn, tx, left,
    load_sem, send1, recv1, send2, recv2, send2x, recv2x, keep_sem, sendq, recvq, relay_sem, row_sem,
):
    n_chan, plane, sig, spec, block, chunks = dims
    part = spec // chunks
    quarters = n_chan // part
    rows = sig // quarters
    me = lax.axis_index("chan")
    gid = lax.axis_index("grp")
    other = lax.rem(gid + plane, 2 * plane)
    y_hi = gid // plane
    x = lax.rem(gid, plane) // 2
    core = lax.rem(gid, 2)
    n_x = plane // 2
    sib = y_hi * plane + x * 2 + (1 - core)
    loads = [
        pltpu.make_async_copy(v_ref, volts, load_sem.at[0]),
        pltpu.make_async_copy(coeff_ref.at[me], coeff, load_sem.at[1]),
        pltpu.make_async_copy(tw_ref, tw, load_sem.at[2]),
        pltpu.make_async_copy(bh_ref, bh, load_sem.at[3]),
        pltpu.make_async_copy(bl_ref, bl, load_sem.at[4]),
    ]
    for item in loads:
        item.start()
    barrier = pltpu.get_barrier_semaphore()

    def greet(k, carry):
        peer = lax.rem(me + k, n_chan)
        pl.semaphore_signal(barrier, inc=1, device_id={"chan": peer}, device_id_type=MESH)
        return carry

    lax.fori_loop(1, n_chan, greet, 0)
    pl.semaphore_signal(barrier, inc=1, device_id={"grp": other}, device_id_type=MESH)
    for dx in range(1, n_x):
        dest = y_hi * plane + lax.rem(x + dx, n_x) * 2 + core
        pl.semaphore_signal(barrier, inc=1, device_id={"grp": dest}, device_id_type=MESH)
    pl.semaphore_signal(barrier, inc=1, device_id={"grp": sib}, device_id_type=MESH)

    loads[1].wait()
    loads[0].wait()

    def widen(lo, hi):
        def body(t, carry):
            vf[t] = volts[t].astype(F32)
            return carry

        lax.fori_loop(lo, hi, body, 0)

    def peer_of(k):
        step = lax.rem(k, 8)
        hop = (step // 2 + 1) * (1 - 2 * lax.rem(step, 2)) * (1 - step // 7)
        z = lax.rem(lax.rem(me, 8) + hop + 8, 8)
        y = lax.rem(me // 8 + k + k // 8, n_chan // 8)
        return y * 8 + z

    def peer_from(k):
        step = lax.rem(k, 8)
        hop = (step // 2 + 1) * (1 - 2 * lax.rem(step, 2)) * (1 - step // 7)
        z = lax.rem(lax.rem(me, 8) - hop + 8, 8)
        y = lax.rem(me // 8 - lax.rem(k + k // 8, n_chan // 8) + n_chan // 8, n_chan // 8)
        return y * 8 + z

    def fir(chunk):
        def body(s, carry):
            for lane in range(0, block, 128):
                lanes = pl.ds(lane, 128)
                total = None
                for t in range(TAPS):
                    term = coeff[t : t + 1, lanes] * vf[chunk * part + s + t, :, lanes]
                    total = term if total is None else total + term
                for q in range(quarters):
                    filt[chunk, quarters * s + q, :, lanes] = total[q * rows : (q + 1) * rows].astype(BF16)
            return carry

        lax.fori_loop(0, part, body, 0)

    def copy1(chunk, src, dest):
        return pltpu.make_async_remote_copy(
            src_ref=filt.at[chunk, dest], dst_ref=r1.at[chunk, src],
            send_sem=send1.at[chunk, dest], recv_sem=recv1.at[chunk, src],
            device_id={"chan": dest}, device_id_type=MESH,
        )

    def start1(chunk):
        def body(k, carry):
            dest = peer_of(k)

            @pl.when(dest != me)
            def _():
                copy1(chunk, me, dest).start()

            return carry

        lax.fori_loop(0, n_chan, body, 0)
        pltpu.make_async_copy(filt.at[chunk, me], r1.at[chunk, me], recv1.at[chunk, me]).start()

    widen(0, part + TAPS - 1)
    def wait1(chunk, lo, hi):
        def body(k, carry):
            d = peer_from(k)
            pltpu.make_async_copy(r1.at[chunk, d], r1.at[chunk, d], recv1.at[chunk, d]).wait()
            return carry

        lax.fori_loop(lo, hi, body, 0)

    widen(0, part + TAPS - 1)
    fir(0)
    pl.semaphore_wait(barrier, n_chan + n_x)
    pl.semaphore_signal(row_sem, inc=1, device_id={"grp": other}, device_id_type=MESH)
    start1(0)
    widen(part + TAPS - 1, spec + TAPS - 1)
    fir(1)
    for item in loads[2:]:
        item.wait()
    start1(1)
    wait1(0, 0, n_chan)

    n_half = n_chan // 2

    def copy2(chunk, src, dest):
        return pltpu.make_async_remote_copy(
            src_ref=s2.at[chunk, dest], dst_ref=r2.at[chunk, src],
            send_sem=send2.at[chunk, dest], recv_sem=recv2.at[chunk, src],
            device_id={"chan": dest}, device_id_type=MESH,
        )

    def copy2x(chunk, src, dest):
        return pltpu.make_async_remote_copy(
            src_ref=s2.at[chunk, dest, 1 - y_hi], dst_ref=r2x.at[chunk, src],
            send_sem=send2x.at[chunk, dest], recv_sem=recv2x.at[chunk, src],
            device_id={"grp": other, "chan": dest}, device_id_type=MESH,
        )

    def transform(chunk):
        def first(p, carry):
            lane = pl.multiple_of(p * 128, 128)
            samples = [r1[chunk, d, :, pl.ds(lane, 128)].astype(F32) for d in range(n_chan)]
            for c, (re, im) in enumerate(real_dft(samples)):
                cos = tw[c, 0:1, pl.ds(lane, 128)]
                sin = tw[c, 1:2, pl.ds(lane, 128)]
                if im is None:
                    zr, zi = re * cos, -(re * sin)
                else:
                    zr, zi = re * cos + im * sin, im * cos - re * sin
                for base, z in ((0, zr), (block, zi)):
                    lanes = pl.ds(pl.multiple_of(base + lane, 128), 128)
                    high = z.astype(BF16)
                    zh[c, :, lanes] = high
                    zl[c, :, lanes] = (z - high.astype(F32)).astype(BF16)
            return carry

        lax.fori_loop(0, block // 128, first, 0)
        count = (n_half + 1) * rows
        left_h = zh[...].reshape(count, 2 * block)
        left_l = zl[...].reshape(count, 2 * block)
        out = jnp.dot(left_h, bh[...], preferred_element_type=F32)
        out += jnp.dot(left_h, bl[...], preferred_element_type=F32)
        out += jnp.dot(left_l, bh[...], preferred_element_type=F32)
        for c in range(n_half + 1):
            piece = out[c * rows : (c + 1) * rows].astype(BF16)
            s2[chunk, c, 0] = piece[:, 0:128]
            s2[chunk, c, 1] = piece[:, 128:256]
            if 0 < c < n_half:
                s2[chunk, n_chan - c, 0] = piece[:, 256:384]
                s2[chunk, n_chan - c, 1] = piece[:, 384:512]

    def start2x(chunk):
        def body(k, carry):
            copy2x(chunk, me, peer_of(k)).start()
            return carry

        lax.fori_loop(0, n_chan, body, 0)

    def start2(chunk):
        def body(k, carry):
            dest = peer_of(k)

            @pl.when(dest != me)
            def _():
                copy2(chunk, me, dest).start()

            return carry

        lax.fori_loop(0, n_chan, body, 0)
        pltpu.make_async_copy(s2.at[chunk, me], r2.at[chunk, me], recv2.at[chunk, me]).start()

    low_lane = lax.broadcasted_iota(jnp.int32, (sig, 128), 1) < 64

    def swap(a, b):
        re = jnp.where(low_lane, a, pltpu.roll(b, 64, 1))
        im = jnp.where(low_lane, pltpu.roll(a, 64, 1), b)
        return jnp.concatenate([re, im], 0).T

    def copyq(src_ref, chunk, slot, sem, dest_grp):
        return pltpu.make_async_remote_copy(
            src_ref=src_ref, dst_ref=slots_ref.at[slot, chunk], send_sem=sem, recv_sem=recvq.at[chunk, slot],
            device_id={"grp": dest_grp}, device_id_type=MESH,
        )

    half_rows = 64 * part
    sends = []
    relays = []

    def own_blocks(chunk):
        def turn(s, carry):
            for q in range(quarters):
                e = quarters * s + q
                pltpu.make_async_copy(r2.at[chunk, e], r2.at[chunk, e], recv2.at[chunk, e]).wait()
            low = r2[chunk, pl.ds(quarters * s, quarters), 0].reshape(sig, 128).astype(F32)
            high = r2[chunk, pl.ds(quarters * s, quarters), 1].reshape(sig, 128).astype(F32)
            t32[chunk, pl.ds(s, 128, stride=part), :] = swap(low, high)
            return carry

        lax.fori_loop(0, part, turn, 0)

        def pack(i, carry):
            at = pl.ds(pl.multiple_of(i * 128, 128), 128)
            tn[chunk, at] = t32[chunk, at, :].astype(BF16)
            return carry

        lax.fori_loop(0, 2 * half_rows // 128, pack, 0)
        for dx in range(1, n_x):
            dest_x = lax.rem(x + dx, n_x)
            dest = y_hi * plane + dest_x * 2 + core
            upper = (dest_x > x).astype(jnp.int32)
            sends.append(copyq(
                tn.at[chunk, pl.ds(pl.multiple_of(upper * half_rows, half_rows), half_rows)],
                chunk, gid, sendq.at[chunk, dx - 1], dest,
            ))
            sends[-1].start()
        sends.append(copyq(
            tn.at[chunk, pl.ds(pl.multiple_of((1 - core) * half_rows, half_rows), half_rows)],
            chunk, gid, sendq.at[chunk, n_x - 1], sib,
        ))
        sends[-1].start()

    def cross_blocks(chunk):
        def turnx(i, carry):
            for q in range(2 * quarters):
                e = 2 * quarters * i + q
                pltpu.make_async_copy(r2x.at[chunk, e], r2x.at[chunk, e], recv2x.at[chunk, e]).wait()
            first_s = r2x[chunk, pl.ds(2 * quarters * i, quarters)].reshape(sig, 128).astype(F32)
            second_s = r2x[chunk, pl.ds(2 * quarters * i + quarters, quarters)].reshape(sig, 128).astype(F32)
            both = swap(first_s, second_s)
            t32x[pl.ds(2 * i, 64, stride=part), :] = both[:64]
            t32x[pl.ds(2 * i + 1, 64, stride=part), :] = both[64:]
            return carry

        lax.fori_loop(0, part // 2, turnx, 0)

        def packx(i, carry):
            at = pl.ds(pl.multiple_of(i * 128, 128), 128)
            tx[chunk, at] = t32x[at, :].astype(BF16)
            return carry

        lax.fori_loop(0, half_rows // 128, packx, 0)
        for dx in range(1, n_x):
            dest = y_hi * plane + lax.rem(x + dx, n_x) * 2 + core
            sends.append(copyq(tx.at[chunk], chunk, other, sendq.at[chunk, n_x + dx - 1], dest))
            sends[-1].start()
        sends.append(copyq(tx.at[chunk], chunk, other, sendq.at[chunk, 2 * n_x - 1], sib))
        sends[-1].start()
        pltpu.make_async_copy(tx.at[chunk], slots_ref.at[other, chunk], recvq.at[chunk, other]).start()

    def relay(chunk, side):
        for dx in (1, 3, 2):
            source = lax.rem(y_hi + side, 2) * plane + lax.rem(x + n_x - dx, n_x) * 2 + core
            copyq(tx.at[chunk], chunk, source, keep_sem, sib).wait_recv()
            relays.append(copyq(
                slots_ref.at[source, chunk], chunk, source,
                relay_sem.at[chunk, side * (n_x - 1) + dx - 1], sib,
            ))
            relays[-1].start()

    transform(0)
    pl.semaphore_wait(row_sem, 1)
    start2x(0)
    start2(0)
    wait1(1, 0, n_chan)
    transform(1)
    cross_blocks(0)
    start2x(1)
    own_blocks(0)
    start2(1)
    relay(0, 1)
    cross_blocks(1)
    own_blocks(1)
    relay(0, 0)

    per = 8 * part

    def prepare(b, carry):
        at = pl.ds(pl.multiple_of(b * per, per), per)
        both = jnp.concatenate([t32[chunk, at, :] for chunk in range(chunks)], 0).T.astype(BF16)
        left[b, :, 0:128] = both[:64]
        left[b, :, 128:256] = both[64:]
        return carry

    lax.fori_loop(0, 16, prepare, 0)
    keep = pltpu.make_async_copy(left, left_ref, keep_sem)
    keep.start()

    relay(chunks - 1, 1)
    relay(chunks - 1, 0)
    for chunk in range(chunks):
        for side in range(2):
            for dx in range(n_x):
                slot = lax.rem(y_hi + side, 2) * plane + lax.rem(x + dx, n_x) * 2 + (1 - core)
                copyq(tx.at[chunk], chunk, slot, keep_sem, sib).wait_recv()
        pltpu.make_async_copy(tx.at[chunk], slots_ref.at[other, chunk], recvq.at[chunk, other]).wait()
    keep.wait()
    for item in sends + relays:
        item.wait_send()

    for chunk in range(chunks):
        def drain(k, carry):
            dest = lax.rem(me + k, n_chan)

            @pl.when(k > 0)
            def _():
                copy1(chunk, me, dest).wait_send()
                copy2(chunk, me, dest).wait_send()

            copy2x(chunk, me, dest).wait_send()
            return carry

        lax.fori_loop(0, n_chan, drain, 0)


def correlate_kernel(
    chunks, spec, plan_ref, left_ref, slots_ref, out_ref, mine, theirs, out, wide, left, left_sem, slot_sem, out_sem
):
    rounds = out.shape[0]
    part = spec // chunks
    per = 8 * part
    gid = lax.axis_index("grp")
    load = pltpu.make_async_copy(left_ref, mine, left_sem)
    load.start()
    fetches = []
    for r in range(rounds):
        fetches.append(pltpu.make_async_copy(slots_ref.at[plan_ref[r, gid]], theirs.at[r], slot_sem.at[r]))
        fetches[-1].start()
    lane_j = lax.rem(lax.broadcasted_iota(jnp.int32, (8, 128), 1), per) // part
    mask = lane_j == lax.broadcasted_iota(jnp.int32, (8, 128), 0)
    low_lane = lax.broadcasted_iota(jnp.int32, (128, 128), 1) < 64
    load.wait()

    def store(r, i):
        at = pl.ds(pl.multiple_of(i * 16, 16), 16)
        return pltpu.make_async_copy(out.at[r, :, at], out_ref.at[r, :, at], out_sem.at[r, i])

    for r in range(rounds):
        fetches[r].wait()

    def step(i, carry):
        for u in range(2):
            for b in range(2):
                wide[...] = mine[u * 8 + 2 * i + b].astype(F32)
                for a in range(0, 64, 2):
                    for lane in (0, 128):
                        pair = [
                            jnp.where(mask, jnp.broadcast_to(wide[a + k : a + k + 1, lane : lane + 128], (8, 128)), 0.0)
                            for k in range(2)
                        ]
                        left[u, b, 8 * a : 8 * a + 16, lane : lane + 128] = jnp.concatenate(pair, 0).astype(BF16)
        for r in range(rounds):
            u = (gid > plan_ref[r, gid]).astype(jnp.int32)
            results = []
            for b in range(2):
                at = pl.ds(pl.multiple_of((2 * i + b) * per, per), per)
                stack = jnp.concatenate([theirs[r, c, at, :] for c in range(chunks)], 0).astype(F32) * (1.0 / spec)
                right = jnp.concatenate(
                    [jnp.where(low_lane, stack, -stack), pltpu.roll(stack, 64, 1)], 0
                ).astype(BF16)
                product = jnp.dot(left[u, b], right, preferred_element_type=F32)
                results.append(product.reshape(64, 8, 128))
            out[r, :, pl.ds(pl.multiple_of(i * 16, 16), 16), :] = jnp.concatenate(results, 1).astype(BF16)
            store(r, i).start()
        return carry

    lax.fori_loop(0, 4, step, 0)
    for r in range(rounds):
        for i in range(4):
            store(r, i).wait()


def solution(mesh):
    n_chan = mesh.shape["chan"]
    n_grp = mesh.shape["grp"]
    plane = n_grp // 2
    n_x = plane // 2
    chunks = 2

    def local(voltages, plan):
        sig, frames, block = voltages.shape
        spec = frames - TAPS + 1
        part = spec // chunks
        fft_len = block * n_chan
        rows = sig * part // n_chan
        n_c = n_chan // 2 + 1
        rounds = plan.shape[0]
        table = jnp.asarray(coeff_table(fft_len, n_chan))
        twiddle = jnp.asarray(twiddle_table(fft_len, n_chan))
        high, low = second_matrix(fft_len, block)
        anyspace = pl.BlockSpec(memory_space=pl.ANY)
        dma = pltpu.SemaphoreType.DMA
        left, slots = pl.pallas_call(
            functools.partial(exchange_kernel, (n_chan, plane, sig, spec, block, chunks)),
            out_shape=(
                jax.ShapeDtypeStruct((16, 64, 256), BF16),
                jax.ShapeDtypeStruct((n_grp, chunks, 64 * part, 128), BF16),
            ),
            in_specs=[anyspace] * 5,
            out_specs=(anyspace, anyspace),
            scratch_shapes=[
                pltpu.VMEM((frames, sig, block), jnp.int32),
                pltpu.VMEM((frames, sig, block), F32),
                pltpu.VMEM((TAPS, block), F32),
                pltpu.VMEM((n_c, 2, block), F32),
                pltpu.VMEM((2 * block, 2 * block), BF16),
                pltpu.VMEM((2 * block, 2 * block), BF16),
                pltpu.VMEM((chunks, n_chan, rows, block), BF16),
                pltpu.VMEM((chunks, n_chan, rows, block), BF16),
                pltpu.VMEM((n_c, rows, 2 * block), BF16),
                pltpu.VMEM((n_c, rows, 2 * block), BF16),
                pltpu.VMEM((chunks, n_chan, 2, rows, 128), BF16),
                pltpu.VMEM((chunks, n_chan, 2, rows, 128), BF16),
                pltpu.VMEM((chunks, n_chan, rows, 128), BF16),
                pltpu.VMEM((chunks, 128 * part, 128), F32),
                pltpu.VMEM((64 * part, 128), F32),
                pltpu.VMEM((chunks, 128 * part, 128), BF16),
                pltpu.VMEM((chunks, 64 * part, 128), BF16),
                pltpu.VMEM((16, 64, 256), BF16),
                dma((5,)),
                dma((chunks, n_chan)), dma((chunks, n_chan)), dma((chunks, n_chan)),
                dma((chunks, n_chan)), dma((chunks, n_chan)), dma((chunks, n_chan)),
                dma, dma((chunks, 2 * n_x)), dma((chunks, n_grp)), dma((chunks, 2 * n_x)),
                pltpu.SemaphoreType.REGULAR,
            ],
            compiler_params=pltpu.CompilerParams(
                collective_id=0, has_side_effects=True, vmem_limit_bytes=56 * 1024 * 1024
            ),
            cost_estimate=pl.CostEstimate(
                flops=10**9, bytes_accessed=10**7, transcendentals=0
            ),
        )(voltages.transpose(1, 0, 2), table, twiddle, jnp.asarray(high), jnp.asarray(low))
        return pl.pallas_call(
            functools.partial(correlate_kernel, chunks, spec),
            out_shape=jax.ShapeDtypeStruct((rounds, sig, 64, 2 * sig), BF16),
            in_specs=[pl.BlockSpec(memory_space=pltpu.SMEM), anyspace, anyspace],
            out_specs=anyspace,
            scratch_shapes=[
                pltpu.VMEM((16, 64, 256), BF16),
                pltpu.VMEM((rounds, chunks, 64 * part, 128), BF16),
                pltpu.VMEM((rounds, sig, 64, 128), BF16),
                pltpu.VMEM((64, 256), F32),
                pltpu.VMEM((2, 2, 512, 256), BF16),
                dma, dma((rounds,)), dma((rounds, 4)),
            ],
            compiler_params=pltpu.CompilerParams(vmem_limit_bytes=60 * 1024 * 1024),
        )(plan, left, slots)

    in_specs = (P("grp", None, "chan"), P())
    out_specs = P(None, "grp", "chan", None)
    return jax.shard_map(local, mesh=mesh, in_specs=in_specs, out_specs=out_specs, check_vma=False)
```
